256 devices in a mesh: atom: 32 (over y, z_lo, core), refl: 8 (over z_hi, x).
Axes of the slice: x: 4, y: 4, z: 8 (z_hi: 2, z_lo: 4; z = z_hi * 4 + z_lo), core: 2. Of those that a mesh axis runs over, the one named last changes fastest.
Arguments:
- coords: float32 [3, 8192], P(None, 'atom'), may hold values from -0.5 to 0.5
- weights: float32 [8192], P('atom'), may hold values from 0.5 to 2
- thermal: float32 [8192], P('atom'), may hold values from 0.5 to 8
- angles: float32 [3, 4], replicated, may hold values from -3.140625 to 3.140625
- miller: int32 [3, 8, 4096], P(None, 'refl'), may hold values from -128 to 127, as said below
- observed: float32 [2, 8, 4096], P(None, 'refl', 'atom'), may hold values from -6 to 6
Outputs:
- tfun: float32 [4, 256, 256, 256], P(None, 'refl', 'atom')
The draws below stay inside these ranges and needn't reach their ends.
Inputs may be any that keep to these rules, and one draw needn't show every extreme that they name: `miller`: reflection i of group g has h mod 256 in g * 32 to (g + 1) * 32 - 1 and k mod 256 in j * 8 to (j + 1) * 8 - 1 with j = i // 128; no two reflections have the same (h, k, l) mod 256.
All inputs are finite; a program needn't handle non-finite values.
Results may differ from the reference program's by a relative error of at most 0.0003.
Values sent between devices are 32-bit elements; how exact they have to be, the bound alone decides.
No kernel may reach another device: no remote copies, remote signals or barrier semaphores. Data moves between devices by JAX's collectives and lax.ppermute only.
A program may use at most 320 MiB of HBM per device.

```python
import math
import jax
import jax.numpy as jnp
from jax import lax

G = 256
REFL_DEV = 128
ROT = 4
NATOM = 8192
REFL_GRP = 4096
NREFL = 32768
PLANES_U = 32
PLANES_V = 8
N_ATOM = 32
N_REFL = 8


def draw_miller(key, part):
    total_cells = PLANES_U * PLANES_V * G
    keys = jax.random.split(key, N_REFL * N_ATOM)
    picks = jax.vmap(lambda single: jax.random.permutation(single, total_cells)[:REFL_DEV])(keys)
    picks = picks.reshape(N_REFL, N_ATOM, REFL_DEV)
    first_local = picks // (PLANES_V * G)
    second_local = picks // G % PLANES_V
    third_index = picks % G
    groups = jnp.arange(N_REFL, dtype=jnp.int32)[:, None, None]
    members = jnp.arange(N_ATOM, dtype=jnp.int32)[None, :, None]
    first_index = groups * PLANES_U + first_local
    second_index = members * PLANES_V + second_local

    def signed(values):
        return jnp.where(values >= G // 2, values - G, values)
    stacked = jnp.stack([signed(first_index), signed(second_index), signed(third_index)])
    return stacked.reshape(3, N_REFL, N_ATOM * REFL_DEV).astype(jnp.int32)


def levels(stream_key, dims, cuts, smallest, largest):
    def one(dim, blocks):
        draws = jax.random.uniform(jax.random.fold_in(jax.random.fold_in(stream_key, 6), dim), (blocks,), jnp.float32, smallest / len(cuts), largest / len(cuts))
        return jnp.repeat(jnp.exp(draws), dims[dim] // blocks).reshape((-1,) + (1,) * (len(dims) - dim - 1))

    factor_of = one(*cuts[0])
    for cut in cuts[1:]:
        factor_of = factor_of * one(*cut)
    return factor_of


def gaussian(key, dims, deviation, most, cuts=(), held_as=jnp.bfloat16):
    values = deviation * jax.random.normal(key, dims, jnp.float32)
    if cuts:
        values = values * levels(key, dims, cuts, -0.22, 0.18)
    return jnp.clip(values, -most, most).astype(held_as)


def setup_inputs(seed: int = 0) -> dict:
    key_of = jax.random.split(jax.random.key(seed), 7)
    coords = jnp.clip(jax.random.uniform(key_of[0], (3, NATOM), jnp.float32, -0.5, 0.5) * levels(key_of[0], (3, NATOM), ((1, 32),), -0.4, 0.0), -0.5, 0.5)
    weights = jnp.clip(jnp.exp(math.log(2.0) - 1.3862944 * jax.random.uniform(key_of[1], (NATOM,), jnp.float32) ** levels(key_of[1], (NATOM,), ((0, 32),), -0.2, 0.2)), 0.5, 2.0)
    thermal = jnp.clip(jnp.exp(math.log(8.0) - 2.7725887 * jax.random.uniform(key_of[2], (NATOM,), jnp.float32) ** levels(key_of[2], (NATOM,), ((0, 32),), -0.2, 0.2)), 0.5, 8.0)
    angles = jnp.clip(jax.random.uniform(key_of[3], (3, ROT), jnp.float32, -3.140625, 3.140625), -3.140625, 3.140625)
    miller = draw_miller(jax.random.fold_in(key_of[6], 71), 0)
    observed = gaussian(key_of[5], (2, N_REFL, REFL_GRP), 1.0, 6.0, ((1, 8), (2, 32)), jnp.float32)
    return {"coords": coords, "weights": weights, "thermal": thermal, "angles": angles, "miller": miller, "observed": observed}


TWO_PI = 2.0 * math.pi

def rotations(angle_batch):
    cos_first = jnp.cos(angle_batch[0])
    sin_first = jnp.sin(angle_batch[0])
    cos_tilt = jnp.cos(angle_batch[1])
    sin_tilt = jnp.sin(angle_batch[1])
    cos_last = jnp.cos(angle_batch[2])
    sin_last = jnp.sin(angle_batch[2])
    top_row = [cos_first * cos_tilt * cos_last - sin_first * sin_last, -cos_first * cos_tilt * sin_last - sin_first * cos_last, cos_first * sin_tilt]
    mid_row = [sin_first * cos_tilt * cos_last + cos_first * sin_last, -sin_first * cos_tilt * sin_last + cos_first * cos_last, sin_first * sin_tilt]
    low_row = [-sin_tilt * cos_last, sin_tilt * sin_last, cos_tilt]
    return jnp.stack([jnp.stack(top_row), jnp.stack(mid_row), jnp.stack(low_row)])

def structure_terms(matrices, coords, weights, thermal, indices, atom_scale):
    placed = jnp.einsum('ijb,ja->bia', matrices, coords, precision=lax.Precision.HIGHEST)
    index_float = indices.astype(jnp.float32)
    turns = jnp.einsum('bia,in->ban', placed, index_float, precision=lax.Precision.HIGHEST)
    resolution = lax.optimization_barrier(jnp.sum(index_float * index_float, axis=0)) / float(G * G)
    amplitude = weights[:, None] * jnp.exp(-thermal[:, None] * resolution[None, :])
    phase_angle = TWO_PI * turns
    real_part = lax.optimization_barrier(jnp.sum(amplitude * jnp.cos(phase_angle), axis=1)) * atom_scale
    imag_part = lax.optimization_barrier(jnp.sum(amplitude * jnp.sin(phase_angle), axis=1)) * atom_scale
    return jnp.stack([real_part, imag_part], axis=1)

def reference(coords, weights, thermal, angles, miller, observed):
    atom_scale = 1.0 / math.sqrt(NATOM)
    refl_scale = 1.0 / math.sqrt(NREFL)
    indices = miller.reshape(3, NREFL)
    obs_flat = observed.reshape(2, NREFL)
    cell_index = jnp.mod(indices, G).astype(jnp.int32)
    by_group = jnp.transpose(miller, (1, 0, 2))

    def transform_one(single):
        matrices = rotations(single[:, None])

        def group_terms(group_indices):
            return structure_terms(matrices, coords, weights, thermal, group_indices, atom_scale)[0]
        fcalc = lax.map(group_terms, by_group)
        fcalc = jnp.transpose(fcalc, (1, 0, 2)).reshape(2, NREFL)
        real_part = (obs_flat[0] * fcalc[0] + obs_flat[1] * fcalc[1]) * refl_scale
        imag_part = (obs_flat[1] * fcalc[0] - obs_flat[0] * fcalc[1]) * refl_scale
        zero_grid = jnp.zeros((G, G, G), jnp.float32)
        spectrum = lax.complex(zero_grid, zero_grid)
        spectrum = spectrum.at[cell_index[0], cell_index[1], cell_index[2]].set(lax.complex(real_part, imag_part))
        field = jnp.real(jnp.fft.ifftn(spectrum)) * float(G) ** 3
        return jnp.transpose(field, (1, 2, 0))
    return lax.map(transform_one, jnp.transpose(angles))
```

```python
import functools
import math

import jax
import jax.numpy as jnp
import numpy as np
from jax import lax
from jax.experimental import pallas as pl
from jax.experimental.pallas import tpu as pltpu
from jax.sharding import PartitionSpec as P

G = 256
TILE = 256
LOG2E = math.log2(math.e)

SIN_C = (3.141592640183972, -5.167710090328514, 2.550077659663962, -0.5982921590533228, 0.07765940739590604)
COS_C = (0.9999999534665512, -4.934792858660287, 4.058411913867176, -1.3318801593277205, 0.21969679475921783)


def rotations(angle_batch):
    cos_first = jnp.cos(angle_batch[0])
    sin_first = jnp.sin(angle_batch[0])
    cos_tilt = jnp.cos(angle_batch[1])
    sin_tilt = jnp.sin(angle_batch[1])
    cos_last = jnp.cos(angle_batch[2])
    sin_last = jnp.sin(angle_batch[2])
    top_row = [
        cos_first * cos_tilt * cos_last - sin_first * sin_last,
        -cos_first * cos_tilt * sin_last - sin_first * cos_last,
        cos_first * sin_tilt,
    ]
    mid_row = [
        sin_first * cos_tilt * cos_last + cos_first * sin_last,
        -sin_first * cos_tilt * sin_last + cos_first * cos_last,
        sin_first * sin_tilt,
    ]
    low_row = [-sin_tilt * cos_last, sin_tilt * sin_last, cos_tilt]
    return jnp.stack([jnp.stack(top_row), jnp.stack(mid_row), jnp.stack(low_row)])


def monic(coefs):
    lead = coefs[-1]
    return lead, [c / lead for c in coefs[:-1]]


def horner_monic(u, rest):
    total = u + rest[-1]
    for c in rest[-2::-1]:
        total = total * u + c
    return total


def half_angle(t):
    t = t - jnp.round(t)
    u = t * t
    return t * horner_monic(u, SIN_M), horner_monic(u, COS_M)


SIN_K, SIN_M = monic(SIN_C)
COS_K, COS_M = monic(COS_C)


def sincos_turns(t):
    s, c = half_angle(t)
    return (2.0 * SIN_K * COS_K) * (s * c), 1.0 - (2.0 * SIN_K * SIN_K) * (s * s)


def split2(x):
    hi = x.astype(jnp.bfloat16)
    lo = (x - hi.astype(jnp.float32)).astype(jnp.bfloat16)
    return hi, lo


def phase_kernel(n_in, first, last, scales, *refs):
    lhs_ref, s2_ref, rc_ref = refs[:3]
    atom_refs = refs[3 : 3 + n_in]
    pos = 3 + n_in
    if not first:
        acc_in = refs[pos]
        pos += 1
    if last:
        obs_ref = refs[pos]
        pos += 1
    out_ref = refs[pos]
    pos += 1
    if last:
        acc_ref = refs[pos]
        pos += 1
    else:
        acc_ref = out_ref
    turns_ref = refs[pos]

    if first:
        acc_ref[...] = jnp.zeros_like(acc_ref)
    else:
        acc_ref[...] = acc_in[...]

    rc0, rc1, rc2 = rc_ref[:, 0:1], rc_ref[:, 1:2], rc_ref[:, 2:3]
    lhs = lhs_ref[...]

    for a_ref in atom_refs:

        @pl.loop(0, a_ref.shape[1] // TILE)
        def _(i):
            a = a_ref[:, pl.ds(pl.multiple_of(i * TILE, TILE), TILE)]
            placed = rc0 * a[0:1] + rc1 * a[1:2] + rc2 * a[2:3]
            p1 = placed.astype(jnp.bfloat16)
            rest = placed - p1.astype(jnp.float32)
            p2 = rest.astype(jnp.bfloat16)
            p3 = (rest - p2.astype(jnp.float32)).astype(jnp.bfloat16)
            rhs = jnp.concatenate([p1, p2, p3], axis=0)
            turns_ref[...] = jnp.dot(lhs, rhs, preferred_element_type=jnp.float32)
            for nb in range(16):
                rows = slice(nb * 8, nb * 8 + 8)
                s2 = s2_ref[rows, :]
                amps = []
                for half in range(2):
                    lanes = slice(half * 128, half * 128 + 128)
                    amps.append(a[3:4, lanes] * jnp.exp2(a[4:5, lanes] * s2))
                acc_ref[8, rows, :] += amps[0] + amps[1]
                for r in range(4):
                    ms = mc = None
                    for half in range(2):
                        lanes = slice(half * 128, half * 128 + 128)
                        s, c = half_angle(turns_ref[r * 128 + nb * 8 : r * 128 + nb * 8 + 8, lanes])
                        m = amps[half] * s
                        ms = m * s if ms is None else ms + m * s
                        mc = m * c if mc is None else mc + m * c
                    acc_ref[r, rows, :] += ms
                    acc_ref[4 + r, rows, :] += mc

    if last:
        atom_scale, refl_scale = scales
        sums = [jnp.sum(acc_ref[q].T, axis=0, keepdims=True) for q in range(9)]
        obs0, obs1 = obs_ref[0:1, :], obs_ref[1:2, :]
        reals, imags = [], []
        for r in range(4):
            f_re = (sums[8] - (2.0 * SIN_K * SIN_K) * sums[r]) * atom_scale
            f_im = ((2.0 * SIN_K * COS_K) * sums[4 + r]) * atom_scale
            reals.append((obs0 * f_re + obs1 * f_im) * refl_scale)
            imags.append((obs1 * f_re - obs0 * f_im) * refl_scale)
        out_ref[...] = jnp.concatenate(reals + imags, axis=0)


def phase_call(lhs, s2, rc, atoms, acc, obs, scales):
    first, last = acc is None, obs is not None
    operands = [lhs, s2, rc, *atoms] + ([] if first else [acc]) + ([obs] if last else [])
    acc_shape = (9, 128, 128)
    scratch = [pltpu.VMEM((512, TILE), jnp.float32)]
    if last:
        scratch = [pltpu.VMEM(acc_shape, jnp.float32)] + scratch
    out = jax.ShapeDtypeStruct((8, 128) if last else acc_shape, jnp.float32)
    count = sum(a.shape[1] for a in atoms)
    return pl.pallas_call(
        functools.partial(phase_kernel, len(atoms), first, last, scales),
        out_shape=out,
        in_specs=[pl.BlockSpec(memory_space=pltpu.VMEM)] * len(operands),
        out_specs=pl.BlockSpec(memory_space=pltpu.VMEM),
        scratch_shapes=scratch,
        compiler_params=pltpu.CompilerParams(vmem_limit_bytes=16 << 20),
        cost_estimate=pl.CostEstimate(
            flops=count * 512 * 22, bytes_accessed=1 << 20, transcendentals=count * 128
        ),
        name="phases",
    )(*operands)


def block_id(core, y, x, z_lo, z_hi):
    return (((core * 4 + y) * 4 + x) * 4 + z_lo) * 2 + z_hi


def transform_kernel(own_ref, c_ref, m_ref, tt_ref, d_ref, out_ref, x_ref, z_ref):
    own = own_ref[0]
    own_j = own_ref[1]
    own_g = own_ref[2]
    cells = lax.broadcasted_iota(jnp.int32, (128, 128), 0)
    w_index = lax.broadcasted_iota(jnp.int32, (8, 128), 0) + own_j * 8

    def scatter(b):
        where = own ^ b
        z_hi = where & 1
        z_lo = (where >> 1) & 3
        x = (where >> 3) & 3
        y = (where >> 5) & 3
        core = (where >> 7) & 1
        g = z_hi * 4 + x
        j = (y * 4 + z_lo) * 2 + core
        m = m_ref[b]
        h = (m[0:1] & 255) - g * 32
        k = (m[1:2] & 255) - j * 8
        row = (h >> 1) * 8 + k
        odd = (h & 1).astype(jnp.float32)
        one_hot = jnp.where(cells == row, 1.0, 0.0).astype(jnp.bfloat16)
        product = (m[2:3] * w_index) & 255
        sine, cosine = sincos_turns(product.astype(jnp.float32) * (1.0 / G))
        c = c_ref[b]
        reals, imags = [], []
        for r in range(4):
            re, im = c[r : r + 1], c[4 + r : 5 + r]
            reals.append(re * cosine - im * sine)
            imags.append(re * sine + im * cosine)
        real, imag = jnp.concatenate(reals, axis=0), jnp.concatenate(imags, axis=0)
        value = jnp.concatenate(
            [real * (1.0 - odd), real * odd, imag * (1.0 - odd), imag * odd], axis=0
        )
        rows = jnp.concatenate(split2(value), axis=0)
        both = lax.dot_general(
            one_hot, rows, (((1,), (1,)), ((), ())), preferred_element_type=jnp.float32
        )
        total = both[:, :128] + both[:, 128:]
        x_ref[pl.ds(g * 16, 16), pl.ds(pl.multiple_of(j * 8, 8), 8), :] = total.reshape(16, 8, 128)

    @pl.loop(0, c_ref.shape[0] // 2)
    def _(i):
        scatter(2 * i)
        scatter(2 * i + 1)

    table = jnp.concatenate(
        [tt_ref[q, pl.ds(pl.multiple_of(own_g * 32, 32), 32), :] for q in range(4)], axis=0
    )
    lane = lax.broadcasted_iota(jnp.int32, (32, 128), 1)
    sign = jnp.where(lane < 64, -1.0, 1.0)

    @pl.loop(0, 64)
    def _(i):
        block = jnp.concatenate([x_ref[2 * i], x_ref[2 * i + 1]], axis=1)
        hi, lo = split2(block)
        o1 = jnp.dot(table, hi, preferred_element_type=jnp.float32)
        o2 = jnp.dot(table[:64], lo, preferred_element_type=jnp.float32)
        z = o1[:64] + o1[64:] + o2
        for half in range(2):
            lanes = slice(half * 128, half * 128 + 128)
            combined = z[:32, lanes] + sign * pltpu.roll(z[32:, lanes], 64, 1)
            z_ref[pl.ds(2 * i + half, 32, stride=128), :] = combined

    @pl.loop(0, 4)
    def _(i):
        parts = []
        for q in range(8):
            zv = z_ref[pl.ds(pl.multiple_of((i * 8 + q) * 128, 128), 128), :].T
            parts.append(
                jnp.concatenate([zv[0:32], zv[32:64], zv[64:96], zv[96:128]], axis=1)
            )
        hi, lo = split2(jnp.concatenate(parts, axis=0))
        d_hi, d_lo = d_ref[0], d_ref[1]
        field = (
            jnp.dot(hi, d_hi, preferred_element_type=jnp.float32)
            + jnp.dot(lo, d_hi, preferred_element_type=jnp.float32)
            + jnp.dot(hi, d_lo, preferred_element_type=jnp.float32)
        )
        for q in range(8):
            for r in range(4):
                out_ref[r, i * 8 + q] = field[q * 32 + r * 8 : q * 32 + r * 8 + 8, :]


def split_np(x):
    hi = x.astype(np.float32).astype(jnp.bfloat16)
    lo = (x - hi.astype(np.float64)).astype(np.float32).astype(jnp.bfloat16)
    return hi, lo


def tables():
    index = np.arange(G)
    angle = 2.0 * np.pi * ((index[:, None] * index[None, :]) % G) / G
    cos_hi, cos_lo = split_np(np.cos(angle))
    sin_hi, sin_lo = split_np(np.sin(angle))
    second = np.stack([cos_hi, sin_hi, cos_lo, sin_lo])
    order = np.concatenate([np.arange(0, G, 2), np.arange(1, G, 2)])
    first = np.stack(
        [
            np.concatenate([cos_hi[order], -sin_hi[order]]),
            np.concatenate([cos_lo[order], -sin_lo[order]]),
        ]
    )
    return second, first


def transform_call(own, coefs, miller, second, first):
    vmem = pl.BlockSpec(memory_space=pltpu.VMEM)
    return pl.pallas_call(
        transform_kernel,
        out_shape=jax.ShapeDtypeStruct((4, 32, 8, G), jnp.float32),
        in_specs=[pl.BlockSpec(memory_space=pltpu.SMEM)] + [vmem] * 4,
        out_specs=vmem,
        scratch_shapes=[
            pltpu.VMEM((128, G, 128), jnp.float32),
            pltpu.VMEM((32 * 128, 128), jnp.float32),
        ],
        compiler_params=pltpu.CompilerParams(vmem_limit_bytes=40 << 20),
        name="transform",
    )(own, coefs, miller, second, first)


def swap(x, axis, mask):
    count = lax.axis_size(axis)
    return lax.ppermute(x, axis, [(i, i ^ mask) for i in range(count)])


def spread(x, axis, masks, dim=0):
    return jnp.concatenate([x] + [swap(x, axis, mask) for mask in masks], axis=dim)


def spread_all(x):
    x = spread(x, "refl", (4,))
    x = spread(x, "atom", (2, 4, 6))
    x = spread(x, "refl", (1, 2, 3))
    x = spread(x, "atom", (8, 16, 24))
    return spread(x, "atom", (1,))


def shards(coords, weights, thermal, angles, miller, observed):
    atom_count = lax.axis_size("atom")
    refl_count = lax.axis_size("refl")
    g = lax.axis_index("refl")
    j = lax.axis_index("atom")
    own_count = observed.shape[2]
    scales = (
        1.0 / math.sqrt(coords.shape[1] * atom_count),
        1.0 / math.sqrt(own_count * atom_count * refl_count),
    )
    atoms = jnp.concatenate([coords, weights[None], thermal[None], jnp.zeros_like(coords)], axis=0)
    atoms = spread(atoms, "atom", (1,), 1)
    atoms = spread(atoms, "atom", (2, 4, 6), 1)
    others = [swap(atoms, "atom", mask) for mask in (8, 16, 24)]

    own_miller = lax.dynamic_slice_in_dim(miller[:, 0, :], j * own_count, own_count, 1)
    indices = own_miller.astype(jnp.float32)
    resolution = jnp.sum(indices * indices, axis=0) * (-LOG2E / (G * G))
    s2 = jnp.broadcast_to(resolution[:, None], (own_count, 128))
    lhs = indices.T[None, :, :, None] * jnp.eye(4, dtype=jnp.float32)[:, None, None, :]
    lhs = jnp.pad(lhs.reshape(4 * own_count, 12), ((0, 0), (0, 4)))
    lhs = jnp.concatenate([lhs, lhs, lhs], axis=1).astype(jnp.bfloat16)
    matrices = rotations(angles)
    rc = jnp.transpose(matrices, (0, 2, 1)).reshape(12, 3)
    rc = jnp.pad(rc, ((0, 4), (0, 125)))

    all_miller = spread_all(own_miller[None])
    acc = phase_call(lhs, s2, rc, [atoms], None, None, scales)
    coefs = phase_call(lhs, s2, rc, others, acc, observed[:, 0, :], scales)
    coefs = spread_all(coefs[None])

    z_hi, x = g // 4, g % 4
    y, z_lo, core = j // 8, (j // 2) % 4, j % 2
    own = jnp.stack([block_id(core, y, x, z_lo, z_hi), j, g]).astype(jnp.int32)
    second, first = tables()
    return transform_call(own, coefs, all_miller, second, first)


def solution(mesh):
    placed = (
        P(None, "atom"),
        P("atom"),
        P("atom"),
        P(),
        P(None, "refl", None),
        P(None, "refl", "atom"),
    )
    return jax.shard_map(
        shards, mesh=mesh, in_specs=placed, out_specs=P(None, "refl", "atom", None), check_vma=False
    )
```

```python
import functools
import math

import jax
import jax.numpy as jnp
import numpy as np
from jax import lax
from jax.experimental import pallas as pl
from jax.experimental.pallas import tpu as pltpu
from jax.sharding import PartitionSpec as P

G = 256
TILE = 256
LOG2E = math.log2(math.e)
ROWS = 11

SIN_C = (3.141592640183972, -5.167710090328514, 2.550077659663962, -0.5982921590533228, 0.07765940739590604)
COS_C = (0.9999999534665512, -4.934792858660287, 4.058411913867176, -1.3318801593277205, 0.21969679475921783)


def rotations(angle_batch):
    cos_first = jnp.cos(angle_batch[0])
    sin_first = jnp.sin(angle_batch[0])
    cos_tilt = jnp.cos(angle_batch[1])
    sin_tilt = jnp.sin(angle_batch[1])
    cos_last = jnp.cos(angle_batch[2])
    sin_last = jnp.sin(angle_batch[2])
    top_row = [
        cos_first * cos_tilt * cos_last - sin_first * sin_last,
        -cos_first * cos_tilt * sin_last - sin_first * cos_last,
        cos_first * sin_tilt,
    ]
    mid_row = [
        sin_first * cos_tilt * cos_last + cos_first * sin_last,
        -sin_first * cos_tilt * sin_last + cos_first * cos_last,
        sin_first * sin_tilt,
    ]
    low_row = [-sin_tilt * cos_last, sin_tilt * sin_last, cos_tilt]
    return jnp.stack([jnp.stack(top_row), jnp.stack(mid_row), jnp.stack(low_row)])


def monic(coefs):
    lead = coefs[-1]
    return lead, [c / lead for c in coefs[:-1]]


def horner_monic(u, rest):
    total = u + rest[-1]
    for c in rest[-2::-1]:
        total = total * u + c
    return total


def half_angle(t):
    t = t - jnp.round(t)
    u = t * t
    return t * horner_monic(u, SIN_M), horner_monic(u, COS_M)


SIN_K, SIN_M = monic(SIN_C)
COS_K, COS_M = monic(COS_C)


def sincos_turns(t):
    s, c = half_angle(t)
    return (2.0 * SIN_K * COS_K) * (s * c), 1.0 - (2.0 * SIN_K * SIN_K) * (s * s)


def split2(x):
    hi = x.astype(jnp.bfloat16)
    lo = (x - hi.astype(jnp.float32)).astype(jnp.bfloat16)
    return hi, lo


def phase_kernel(n_in, first, last, scales, *refs):
    lhs_ref, s2_ref, rc_ref = refs[:3]
    atom_refs = refs[3 : 3 + n_in]
    pos = 3 + n_in
    if not first:
        acc_in = refs[pos]
        pos += 1
    if last:
        obs_ref, ind_ref = refs[pos : pos + 2]
        pos += 2
    out_ref = refs[pos]
    pos += 1
    if last:
        acc_ref = refs[pos]
        pos += 1
    else:
        acc_ref = out_ref
    turns_ref = refs[pos]

    if first:
        acc_ref[...] = jnp.zeros_like(acc_ref)
    else:
        acc_ref[...] = acc_in[...]

    rc0, rc1, rc2 = rc_ref[:, 0:1], rc_ref[:, 1:2], rc_ref[:, 2:3]
    lhs = lhs_ref[...]

    for a_ref in atom_refs:

        @pl.loop(0, a_ref.shape[1] // TILE)
        def _(i):
            a = a_ref[:, pl.ds(pl.multiple_of(i * TILE, TILE), TILE)]
            placed = rc0 * a[0:1] + rc1 * a[1:2] + rc2 * a[2:3]
            p1 = placed.astype(jnp.bfloat16)
            rest = placed - p1.astype(jnp.float32)
            p2 = rest.astype(jnp.bfloat16)
            p3 = (rest - p2.astype(jnp.float32)).astype(jnp.bfloat16)
            rhs = jnp.concatenate([p1, p2, p3], axis=0)
            turns_ref[...] = jnp.dot(lhs, rhs, preferred_element_type=jnp.float32)
            for nb in range(16):
                rows = slice(nb * 8, nb * 8 + 8)
                s2 = s2_ref[rows, :]
                amps = []
                for half in range(2):
                    lanes = slice(half * 128, half * 128 + 128)
                    amps.append(a[3:4, lanes] * jnp.exp2(a[4:5, lanes] * s2))
                acc_ref[8, rows, :] += amps[0] + amps[1]
                for r in range(4):
                    ms = mc = None
                    for half in range(2):
                        lanes = slice(half * 128, half * 128 + 128)
                        s, c = half_angle(turns_ref[r * 128 + nb * 8 : r * 128 + nb * 8 + 8, lanes])
                        m = amps[half] * s
                        ms = m * s if ms is None else ms + m * s
                        mc = m * c if mc is None else mc + m * c
                    acc_ref[r, rows, :] += ms
                    acc_ref[4 + r, rows, :] += mc

    if last:
        atom_scale, refl_scale = scales
        sums = [jnp.sum(acc_ref[q].T, axis=0, keepdims=True) for q in range(9)]
        obs0, obs1 = obs_ref[0:1, :], obs_ref[1:2, :]
        reals, imags = [], []
        for r in range(4):
            f_re = (sums[8] - (2.0 * SIN_K * SIN_K) * sums[r]) * atom_scale
            f_im = ((2.0 * SIN_K * COS_K) * sums[4 + r]) * atom_scale
            reals.append((obs0 * f_re + obs1 * f_im) * refl_scale)
            imags.append((obs1 * f_re - obs0 * f_im) * refl_scale)
        for q, row in enumerate(reals + imags + [ind_ref[q : q + 1, :] for q in range(3)]):
            out_ref[0:1, q * 128 : q * 128 + 128] = row


def phase_call(lhs, s2, rc, atoms, acc, obs, indices, scales):
    first, last = acc is None, obs is not None
    operands = [lhs, s2, rc, *atoms] + ([] if first else [acc]) + ([obs, indices] if last else [])
    acc_shape = (9, 128, 128)
    scratch = [pltpu.VMEM((512, TILE), jnp.float32)]
    if last:
        scratch = [pltpu.VMEM(acc_shape, jnp.float32)] + scratch
    out = jax.ShapeDtypeStruct((1, ROWS * 128) if last else acc_shape, jnp.float32)
    count = sum(a.shape[1] for a in atoms)
    return pl.pallas_call(
        functools.partial(phase_kernel, len(atoms), first, last, scales),
        out_shape=out,
        in_specs=[pl.BlockSpec(memory_space=pltpu.VMEM)] * len(operands),
        out_specs=pl.BlockSpec(memory_space=pltpu.VMEM),
        scratch_shapes=scratch,
        compiler_params=pltpu.CompilerParams(vmem_limit_bytes=16 << 20),
        cost_estimate=pl.CostEstimate(
            flops=count * 512 * 22, bytes_accessed=1 << 20, transcendentals=count * 128
        ),
        name="phases",
    )(*operands)


def scatter_kernel(piece, own_ref, p_ref, x_ref):
    y, core = own_ref[0] ^ (piece & 3), own_ref[1] ^ (piece >> 2)
    cells = lax.broadcasted_iota(jnp.int32, (128, 128), 0).astype(jnp.float32)
    w_turn = (lax.broadcasted_iota(jnp.int32, (8, 128), 0) + own_ref[3] * 8).astype(
        jnp.float32
    ) * (1.0 / G)
    sub = lax.broadcasted_iota(jnp.int32, (8, 128), 0)
    for base in range(0, 32, 8):
        h = p_ref[base : base + 8, 8 * 128 : 9 * 128]
        k = p_ref[base : base + 8, 9 * 128 : 10 * 128]
        third = p_ref[base : base + 8, 10 * 128 : 11 * 128]
        h = jnp.where(h < 0.0, h + G, h) - ((base + sub) // 4 * 32).astype(jnp.float32)
        k = jnp.where(k < 0.0, k + G, k) - (((y * 4 + (sub & 3)) * 2 + core) * 8).astype(jnp.float32)
        pair = jnp.floor(h * 0.5)
        odd = h - 2.0 * pair
        row = pair * 8.0 + k
        for q in range(8):
            i = base + q
            g, z_lo = i // 4, i % 4
            one_hot = jnp.where(cells == row[q : q + 1], 1.0, 0.0).astype(jnp.bfloat16)
            sine, cosine = sincos_turns(third[q : q + 1] * w_turn)
            reals, imags = [], []
            for r in range(4):
                re = p_ref[i : i + 1, r * 128 : r * 128 + 128]
                im = p_ref[i : i + 1, (4 + r) * 128 : (5 + r) * 128]
                reals.append(re * cosine - im * sine)
                imags.append(re * sine + im * cosine)
            hi, lo = split2(jnp.concatenate(reals + imags, axis=0))
            odd_row = jnp.broadcast_to(odd[q : q + 1], (32, 128)).astype(jnp.bfloat16)
            even_row = jnp.broadcast_to(1.0 - odd[q : q + 1], (32, 128)).astype(jnp.bfloat16)

            def masked(part):
                return jnp.concatenate(
                    [part[:32] * even_row, part[:32] * odd_row, part[32:] * even_row, part[32:] * odd_row],
                    axis=0,
                )

            total = lax.dot_general(
                jnp.concatenate([one_hot, one_hot], axis=1),
                jnp.concatenate([masked(hi), masked(lo)], axis=1),
                (((1,), (1,)), ((), ())),
                preferred_element_type=jnp.float32,
            )
            x_ref[g * 16 : g * 16 + 16, z_lo * 8 : z_lo * 8 + 8, :] = total.reshape(16, 8, 128)


def scatter_call(piece, own, payload):
    vmem = pl.BlockSpec(memory_space=pltpu.VMEM)
    return pl.pallas_call(
        functools.partial(scatter_kernel, piece),
        out_shape=jax.ShapeDtypeStruct((128, 32, 128), jnp.float32),
        in_specs=[pl.BlockSpec(memory_space=pltpu.SMEM), vmem],
        out_specs=vmem,
        compiler_params=pltpu.CompilerParams(vmem_limit_bytes=16 << 20),
        cost_estimate=pl.CostEstimate(flops=2 << 30, bytes_accessed=1 << 20, transcendentals=0),
        name="scatter",
    )(own, payload)


def transform_kernel(own_ref, *refs):
    x_refs, (d_ref, out_ref, z_ref) = refs[:8], refs[8:]
    own_y, own_core, own_g = own_ref[0], own_ref[1], own_ref[2]
    column = lax.broadcasted_iota(jnp.int32, (32, G), 1)
    y, core = own_y ^ ((column >> 5) & 3), own_core ^ (column >> 7)
    k = ((y * 4 + ((column >> 3) & 3)) * 2 + core) * 8 + (column & 7)
    v = lax.broadcasted_iota(jnp.int32, (32, G), 0) + own_g * 32
    sine, cosine = sincos_turns(((k * v) & (G - 1)).astype(jnp.float32) * (1.0 / G))
    table = jnp.concatenate(split2(jnp.concatenate([cosine, sine], axis=0)), axis=0)
    lane = lax.broadcasted_iota(jnp.int32, (32, 128), 1)
    sign = jnp.where(lane < 64, -1.0, 1.0)

    @pl.loop(0, 64, unroll=8)
    def _(i):
        sides = [jnp.concatenate([x_ref[2 * i + q] for x_ref in x_refs], axis=0) for q in range(2)]
        hi, lo = split2(jnp.concatenate(sides, axis=1))
        o1 = jnp.dot(table, hi, preferred_element_type=jnp.float32)
        o2 = jnp.dot(table[:64], lo, preferred_element_type=jnp.float32)
        z = o1[:64] + o1[64:] + o2
        for half in range(2):
            lanes = slice(half * 128, half * 128 + 128)
            combined = z[:32, lanes] + sign * pltpu.roll(z[32:, lanes], 64, 1)
            z_ref[pl.ds(2 * i + half, 32, stride=128), :] = combined

    @pl.loop(0, 4, unroll=4)
    def _(i):
        parts = []
        for q in range(8):
            zv = z_ref[pl.ds(pl.multiple_of((i * 8 + q) * 128, 128), 128), :].T
            parts.append(
                jnp.concatenate([zv[0:32], zv[32:64], zv[64:96], zv[96:128]], axis=1)
            )
        hi, lo = split2(jnp.concatenate(parts, axis=0))
        d_hi, d_lo = d_ref[0], d_ref[1]
        field = (
            jnp.dot(hi, d_hi, preferred_element_type=jnp.float32)
            + jnp.dot(lo, d_hi, preferred_element_type=jnp.float32)
            + jnp.dot(hi, d_lo, preferred_element_type=jnp.float32)
        )
        for q in range(8):
            for r in range(4):
                out_ref[r, i * 8 + q] = field[q * 32 + r * 8 : q * 32 + r * 8 + 8, :]


def split_np(x):
    hi = x.astype(np.float32).astype(jnp.bfloat16)
    lo = (x - hi.astype(np.float64)).astype(np.float32).astype(jnp.bfloat16)
    return hi, lo


def first_table():
    index = np.arange(G)
    angle = 2.0 * np.pi * ((index[:, None] * index[None, :]) % G) / G
    cos_hi, cos_lo = split_np(np.cos(angle))
    sin_hi, sin_lo = split_np(np.sin(angle))
    order = np.concatenate([np.arange(0, G, 2), np.arange(1, G, 2)])
    return np.stack(
        [
            np.concatenate([cos_hi[order], -sin_hi[order]]),
            np.concatenate([cos_lo[order], -sin_lo[order]]),
        ]
    )


def transform_call(own, pieces, first):
    vmem = pl.BlockSpec(memory_space=pltpu.VMEM)
    return pl.pallas_call(
        transform_kernel,
        out_shape=jax.ShapeDtypeStruct((4, 32, 8, G), jnp.float32),
        in_specs=[pl.BlockSpec(memory_space=pltpu.SMEM)] + [vmem] * 9,
        out_specs=vmem,
        scratch_shapes=[pltpu.VMEM((32 * 128, 128), jnp.float32)],
        compiler_params=pltpu.CompilerParams(vmem_limit_bytes=40 << 20),
        name="transform",
    )(own, *pieces, first)


def swap(x, axis, mask):
    count = lax.axis_size(axis)
    return lax.ppermute(x, axis, [(i, i ^ mask) for i in range(count)])


def column_groups():
    return [
        [((y * 4 + z_lo) * 2 + core) * 8 + g for g in range(8) for z_lo in range(4)]
        for y in range(4)
        for core in range(2)
    ]


def shards(coords, weights, thermal, angles, miller, observed):
    atom_count = lax.axis_size("atom")
    refl_count = lax.axis_size("refl")
    g = lax.axis_index("refl")
    j = lax.axis_index("atom")
    own_count = observed.shape[2]
    scales = (
        1.0 / math.sqrt(coords.shape[1] * atom_count),
        1.0 / math.sqrt(own_count * atom_count * refl_count),
    )
    atoms = jnp.concatenate([coords, weights[None], thermal[None], jnp.zeros_like(coords)], axis=0)
    atoms = jnp.concatenate([atoms, swap(atoms, "atom", 1)], axis=1)
    near = [swap(atoms, "atom", mask) for mask in (2, 6, 4)]
    run = jnp.concatenate([atoms, *near], axis=1)
    far = [swap(run, "atom", mask) for mask in (8, 24, 16)]

    own_miller = lax.dynamic_slice_in_dim(miller[:, 0, :], j * own_count, own_count, 1)
    indices = own_miller.astype(jnp.float32)
    resolution = jnp.sum(indices * indices, axis=0) * (-LOG2E / (G * G))
    s2 = jnp.broadcast_to(resolution[:, None], (own_count, 128))
    lhs = indices.T[None, :, :, None] * jnp.eye(4, dtype=jnp.float32)[:, None, None, :]
    lhs = jnp.pad(lhs.reshape(4 * own_count, 12), ((0, 0), (0, 4)))
    lhs = jnp.concatenate([lhs, lhs, lhs], axis=1).astype(jnp.bfloat16)
    matrices = rotations(angles)
    rc = jnp.transpose(matrices, (0, 2, 1)).reshape(12, 3)
    rc = jnp.pad(rc, ((0, 4), (0, 125)))

    acc = phase_call(lhs, s2, rc, [atoms], None, None, None, scales)
    acc = phase_call(lhs, s2, rc, near, acc, None, None, scales)
    payload = phase_call(lhs, s2, rc, far, acc, observed[:, 0, :], indices, scales)

    own = jnp.stack([j // 8, j % 2, g, j]).astype(jnp.int32)
    plane = lax.all_to_all(
        jnp.broadcast_to(payload, (32, payload.shape[1])),
        ("atom", "refl"),
        0,
        0,
        tiled=True,
        axis_index_groups=column_groups(),
    )
    pieces = [plane] + [None] * 7
    for m in (1, 3, 2):
        pieces[m] = swap(plane, "atom", 8 * m)
    for m in (0, 1, 3, 2):
        pieces[4 + m] = swap(pieces[m], "atom", 1)
    lines = [scatter_call(q, own, piece) for q, piece in enumerate(pieces)]
    return transform_call(own, lines, first_table())


def solution(mesh):
    placed = (
        P(None, "atom"),
        P("atom"),
        P("atom"),
        P(),
        P(None, "refl", None),
        P(None, "refl", "atom"),
    )
    return jax.shard_map(
        shards, mesh=mesh, in_specs=placed, out_specs=P(None, "refl", "atom", None), check_vma=False
    )
```

```python
import functools
import math

import jax
import jax.numpy as jnp
import numpy as np
from jax import lax
from jax.experimental import pallas as pl
from jax.experimental.pallas import tpu as pltpu
from jax.sharding import PartitionSpec as P

G = 256
TILE = 256
LOG2E = math.log2(math.e)
PLANE = 32
ROWS = 11

SIN_C = (3.141592640183972, -5.167710090328514, 2.550077659663962, -0.5982921590533228, 0.07765940739590604)
COS_C = (0.9999999534665512, -4.934792858660287, 4.058411913867176, -1.3318801593277205, 0.21969679475921783)


def rotation_columns(angles):
    cosine, sine = jnp.cos(angles), jnp.sin(angles)
    cos_first, cos_tilt, cos_last = (cosine[:, q : q + 1] for q in range(3))
    sin_first, sin_tilt, sin_last = (sine[:, q : q + 1] for q in range(3))
    top_row = [
        cos_first * cos_tilt * cos_last - sin_first * sin_last,
        -cos_first * cos_tilt * sin_last - sin_first * cos_last,
        cos_first * sin_tilt,
    ]
    mid_row = [
        sin_first * cos_tilt * cos_last + cos_first * sin_last,
        -sin_first * cos_tilt * sin_last + cos_first * cos_last,
        sin_first * sin_tilt,
    ]
    low_row = [-sin_tilt * cos_last, sin_tilt * sin_last, cos_tilt]
    row = lax.broadcasted_iota(jnp.int32, (16, 1), 0)
    low_row = [jnp.where(row < 12, low, 0.0) for low in low_row]
    return [
        jnp.where(row < 4, top, jnp.where(row < 8, mid, low))
        for top, mid, low in zip(top_row, mid_row, low_row)
    ]


def monic(coefs):
    lead = coefs[-1]
    return lead, [c / lead for c in coefs[:-1]]


def horner_monic(u, rest):
    total = u + rest[-1]
    for c in rest[-2::-1]:
        total = total * u + c
    return total


def half_angle(t):
    t = t - jnp.round(t)
    u = t * t
    return t * horner_monic(u, SIN_M), horner_monic(u, COS_M)


SIN_K, SIN_M = monic(SIN_C)
COS_K, COS_M = monic(COS_C)


def sincos_turns(t):
    s, c = half_angle(t)
    return (2.0 * SIN_K * COS_K) * (s * c), 1.0 - (2.0 * SIN_K * SIN_K) * (s * s)


def split2(x):
    hi = x.astype(jnp.bfloat16)
    lo = (x - hi.astype(jnp.float32)).astype(jnp.bfloat16)
    return hi, lo


def phase_kernel(n_in, skip, first, last, scales, *refs):
    lhs_ref, s2_ref, rc_ref = refs[:3]
    atom_refs = refs[3 : 3 + n_in]
    pos = 3 + n_in
    if not first:
        acc_in = refs[pos]
        pos += 1
    if last:
        obs_ref, ind_ref = refs[pos : pos + 2]
        pos += 2
    out_ref = refs[pos]
    pos += 1
    if first:
        rc_out = refs[pos]
        pos += 1
    if last:
        acc_ref = refs[pos]
        pos += 1
    else:
        acc_ref = out_ref
    even_ref, odd_ref = refs[pos : pos + 2]

    if first:
        acc_ref[...] = jnp.zeros_like(acc_ref)
    else:
        acc_ref[...] = acc_in[...]

    if first:
        rc0, rc1, rc2 = rotation_columns(rc_ref[...])
        for q, column in enumerate((rc0, rc1, rc2)):
            rc_out[:, q : q + 1] = column
    else:
        rc0, rc1, rc2 = rc_ref[:, 0:1], rc_ref[:, 1:2], rc_ref[:, 2:3]
    lhs = lhs_ref[...]

    def set_turns(a_ref, i, turns_ref):
        a = a_ref[:, pl.ds(pl.multiple_of(i * TILE, TILE), TILE)]
        placed = rc0 * a[0:1] + rc1 * a[1:2] + rc2 * a[2:3]
        p1 = placed.astype(jnp.bfloat16)
        rest = placed - p1.astype(jnp.float32)
        p2 = rest.astype(jnp.bfloat16)
        p3 = (rest - p2.astype(jnp.float32)).astype(jnp.bfloat16)
        rhs = jnp.concatenate([p1, p2, p3], axis=0)
        turns_ref[...] = jnp.dot(lhs, rhs, preferred_element_type=jnp.float32)

    def add_tile(a_ref, i, turns_ref):
        a = a_ref[:, pl.ds(pl.multiple_of(i * TILE, TILE), TILE)]
        for nb in range(16):
            rows = slice(nb * 8, nb * 8 + 8)
            s2 = s2_ref[rows, :]
            amps = []
            for part in range(TILE // 128):
                lanes = slice(part * 128, part * 128 + 128)
                amps.append(a[3:4, lanes] * jnp.exp2(a[4:5, lanes] * s2))
            acc_ref[8, rows, :] += sum(amps[1:], amps[0])
            for r in range(4):
                ms = mc = None
                for part in range(TILE // 128):
                    lanes = slice(part * 128, part * 128 + 128)
                    s, c = half_angle(turns_ref[r * 128 + nb * 8 : r * 128 + nb * 8 + 8, lanes])
                    m = amps[part] * s
                    ms = m * s if ms is None else ms + m * s
                    mc = m * c if mc is None else mc + m * c
                acc_ref[r, rows, :] += ms
                acc_ref[4 + r, rows, :] += mc

    for a_ref in atom_refs:
        begin, tiles = skip // TILE, a_ref.shape[1] // TILE
        set_turns(a_ref, begin, even_ref)
        if tiles == begin + 1:
            add_tile(a_ref, begin, even_ref)
        else:

            @pl.loop(begin // 2, tiles // 2)
            def _(i):
                set_turns(a_ref, 2 * i + 1, odd_ref)
                add_tile(a_ref, 2 * i, even_ref)
                set_turns(a_ref, jnp.minimum(2 * i + 2, tiles - 1), even_ref)
                add_tile(a_ref, 2 * i + 1, odd_ref)

    if last:
        atom_scale, refl_scale = scales
        sums = [jnp.sum(acc_ref[q].T, axis=0, keepdims=True) for q in range(9)]
        obs0, obs1 = obs_ref[0:1, :], obs_ref[1:2, :]
        reals, imags = [], []
        for r in range(4):
            f_re = (sums[8] - (2.0 * SIN_K * SIN_K) * sums[r]) * atom_scale
            f_im = ((2.0 * SIN_K * COS_K) * sums[4 + r]) * atom_scale
            reals.append((obs0 * f_re + obs1 * f_im) * refl_scale)
            imags.append((obs1 * f_re - obs0 * f_im) * refl_scale)
        for q, row in enumerate(reals + imags + [ind_ref[q : q + 1, :] for q in range(3)]):
            out_ref[:, q * 128 : q * 128 + 128] = jnp.broadcast_to(row, (out_ref.shape[0], 128))


def phase_call(lhs, s2, rc, atoms, skip, acc, obs, indices, scales):
    first, last = acc is None, obs is not None
    operands = [lhs, s2, rc, *atoms] + ([] if first else [acc]) + ([obs, indices] if last else [])
    acc_shape = (9, 128, 128)
    scratch = [pltpu.VMEM((512, TILE), jnp.float32)] * 2
    if last:
        scratch = [pltpu.VMEM(acc_shape, jnp.float32)] + scratch
    vmem = pl.BlockSpec(memory_space=pltpu.VMEM)
    out, out_specs = jax.ShapeDtypeStruct((PLANE, ROWS * 128) if last else acc_shape, jnp.float32), vmem
    if first:
        out, out_specs = (out, jax.ShapeDtypeStruct((16, 128), jnp.float32)), (vmem, vmem)
    count = sum(a.shape[1] for a in atoms) - skip
    return pl.pallas_call(
        functools.partial(phase_kernel, len(atoms), skip, first, last, scales),
        out_shape=out,
        in_specs=[vmem] * len(operands),
        out_specs=out_specs,
        scratch_shapes=scratch,
        compiler_params=pltpu.CompilerParams(vmem_limit_bytes=16 << 20),
        cost_estimate=pl.CostEstimate(
            flops=count * 512 * 22, bytes_accessed=1 << 20, transcendentals=count * 128
        ),
        name="phases",
    )(*operands)


def scatter_kernel(other, step, own_ref, p_ref, x_ref):
    core, y, own_j = own_ref[0:1] ^ other, own_ref[3:4] ^ step, own_ref[2:3]
    cells = lax.broadcasted_iota(jnp.int32, (128, 128), 0).astype(jnp.float32)
    w_turn = (lax.broadcasted_iota(jnp.int32, (8, 128), 0) + own_j * 8).astype(
        jnp.float32
    ) * (1.0 / G)
    sub = lax.broadcasted_iota(jnp.int32, (8, 128), 0)
    for base in range(0, PLANE, 8):
        x = base // 8
        h = p_ref[base : base + 8, 8 * 128 : 9 * 128]
        k = p_ref[base : base + 8, 9 * 128 : 10 * 128]
        third = p_ref[base : base + 8, 10 * 128 : 11 * 128]
        h = jnp.where(h < 0.0, h + G, h) - (((sub >> 2) * 4 + x) * 32).astype(jnp.float32)
        k = jnp.where(k < 0.0, k + G, k) - (((y * 4 + (sub & 3)) * 2 + core) * 8).astype(jnp.float32)
        pair = jnp.floor(h * 0.5)
        odd = h - 2.0 * pair
        row = pair * 8.0 + k
        for q in range(8):
            i = base + q
            g, line = q // 4 * 4 + x, q % 4 * 8
            one_hot = jnp.where(cells == row[q : q + 1], 1.0, 0.0).astype(jnp.bfloat16)
            sine, cosine = sincos_turns(third[q : q + 1] * w_turn)
            reals, imags = [], []
            for r in range(4):
                re = p_ref[i : i + 1, r * 128 : r * 128 + 128]
                im = p_ref[i : i + 1, (4 + r) * 128 : (5 + r) * 128]
                reals.append(re * cosine - im * sine)
                imags.append(re * sine + im * cosine)
            hi, lo = split2(jnp.concatenate(reals + imags, axis=0))
            odd_row = jnp.broadcast_to(odd[q : q + 1], (32, 128)).astype(jnp.bfloat16)
            even_row = jnp.broadcast_to(1.0 - odd[q : q + 1], (32, 128)).astype(jnp.bfloat16)

            def masked(part):
                return jnp.concatenate(
                    [part[:32] * even_row, part[:32] * odd_row, part[32:] * even_row, part[32:] * odd_row],
                    axis=0,
                )

            total = lax.dot_general(
                jnp.concatenate([one_hot, one_hot], axis=1),
                jnp.concatenate([masked(hi), masked(lo)], axis=1),
                (((1,), (1,)), ((), ())),
                preferred_element_type=jnp.float32,
            )
            x_ref[g * 16 : g * 16 + 16, line : line + 8, :] = total.reshape(16, 8, 128)


def scatter_call(other, step, own, plane):
    vmem = pl.BlockSpec(memory_space=pltpu.VMEM)
    return pl.pallas_call(
        functools.partial(scatter_kernel, other, step),
        out_shape=jax.ShapeDtypeStruct((128, 32, 128), jnp.float32),
        in_specs=[vmem] * 2,
        out_specs=vmem,
        compiler_params=pltpu.CompilerParams(vmem_limit_bytes=16 << 20),
        cost_estimate=pl.CostEstimate(flops=1 << 29, bytes_accessed=1 << 20, transcendentals=0),
        name="scatter",
    )(own, plane)


def transform_kernel(own_ref, *refs):
    x_refs, (d_ref, out_ref, z_ref) = refs[:8], refs[8:]
    own_core, own_g, own_y = (jnp.concatenate([own_ref[q : q + 1]] * 2, axis=1) for q in (0, 1, 3))
    column = lax.broadcasted_iota(jnp.int32, (32, G), 1)
    y, core = own_y ^ ((column >> 5) & 3), own_core ^ (column >> 7)
    k = ((y * 4 + ((column >> 3) & 3)) * 2 + core) * 8 + (column & 7)
    v = lax.broadcasted_iota(jnp.int32, (32, G), 0) + own_g * 32
    sine, cosine = sincos_turns(((k * v) & (G - 1)).astype(jnp.float32) * (1.0 / G))
    table = jnp.concatenate(split2(jnp.concatenate([cosine, sine], axis=0)), axis=0)
    lane = lax.broadcasted_iota(jnp.int32, (32, 128), 1)
    sign = jnp.where(lane < 64, -1.0, 1.0)

    @pl.loop(0, 64, unroll=8)
    def _(i):
        sides = [jnp.concatenate([x_ref[2 * i + q] for x_ref in x_refs], axis=0) for q in range(2)]
        hi, lo = split2(jnp.concatenate(sides, axis=1))
        o1 = jnp.dot(table, hi, preferred_element_type=jnp.float32)
        o2 = jnp.dot(table[:64], lo, preferred_element_type=jnp.float32)
        z = o1[:64] + o1[64:] + o2
        for half in range(2):
            lanes = slice(half * 128, half * 128 + 128)
            combined = z[:32, lanes] + sign * pltpu.roll(z[32:, lanes], 64, 1)
            z_ref[pl.ds(2 * i + half, 32, stride=128), :] = combined

    @pl.loop(0, 4, unroll=4)
    def _(i):
        parts = []
        for q in range(8):
            zv = z_ref[pl.ds(pl.multiple_of((i * 8 + q) * 128, 128), 128), :].T
            parts.append(
                jnp.concatenate([zv[0:32], zv[32:64], zv[64:96], zv[96:128]], axis=1)
            )
        hi, lo = split2(jnp.concatenate(parts, axis=0))
        d_hi, d_lo = d_ref[0], d_ref[1]
        field = (
            jnp.dot(hi, d_hi, preferred_element_type=jnp.float32)
            + jnp.dot(lo, d_hi, preferred_element_type=jnp.float32)
            + jnp.dot(hi, d_lo, preferred_element_type=jnp.float32)
        )
        for q in range(8):
            for r in range(4):
                out_ref[r, i * 8 + q] = field[q * 32 + r * 8 : q * 32 + r * 8 + 8, :]


def split_np(x):
    hi = x.astype(np.float32).astype(jnp.bfloat16)
    lo = (x - hi.astype(np.float64)).astype(np.float32).astype(jnp.bfloat16)
    return hi, lo


def first_table():
    index = np.arange(G)
    angle = 2.0 * np.pi * ((index[:, None] * index[None, :]) % G) / G
    cos_hi, cos_lo = split_np(np.cos(angle))
    sin_hi, sin_lo = split_np(np.sin(angle))
    order = np.concatenate([np.arange(0, G, 2), np.arange(1, G, 2)])
    return np.stack(
        [
            np.concatenate([cos_hi[order], -sin_hi[order]]),
            np.concatenate([cos_lo[order], -sin_lo[order]]),
        ]
    )


def transform_call(own, pieces, first):
    vmem = pl.BlockSpec(memory_space=pltpu.VMEM)
    return pl.pallas_call(
        transform_kernel,
        out_shape=jax.ShapeDtypeStruct((4, 32, 8, G), jnp.float32),
        in_specs=[vmem] * 10,
        out_specs=vmem,
        scratch_shapes=[pltpu.VMEM((32 * 128, 128), jnp.float32)],
        compiler_params=pltpu.CompilerParams(vmem_limit_bytes=8 << 20),
        name="transform",
    )(own, *pieces, first)


def swap(x, axis, mask):
    count = lax.axis_size(axis)
    return lax.ppermute(x, axis, [(i, i ^ mask) for i in range(count)])


def flat(y, z, core, x):
    return ((y * 4 + z % 4) * 2 + core) * 8 + z // 4 * 4 + x


def plane_groups():
    return [
        [flat(y, z, core, x) for x in range(4) for z in range(8)] for y in range(4) for core in range(2)
    ]


def join_kernel(a_ref, b_ref, out_ref):
    size = a_ref.shape[1]
    out_ref[:, :size] = a_ref[...]
    out_ref[:, size:] = b_ref[...]


def join(a, b):
    vmem = pl.BlockSpec(memory_space=pltpu.VMEM)
    return pl.pallas_call(
        join_kernel,
        out_shape=jax.ShapeDtypeStruct((a.shape[0], 2 * a.shape[1]), jnp.float32),
        in_specs=[vmem, vmem],
        out_specs=vmem,
        compiler_params=pltpu.CompilerParams(vmem_limit_bytes=4 << 20),
        name="join",
    )(a, b)


def shards(coords, weights, thermal, angles, miller, observed):
    atom_count = lax.axis_size("atom")
    refl_count = lax.axis_size("refl")
    g = lax.axis_index("refl")
    j = lax.axis_index("atom")
    own_count = observed.shape[2]
    scales = (
        1.0 / math.sqrt(coords.shape[1] * atom_count),
        1.0 / math.sqrt(own_count * atom_count * refl_count),
    )
    atoms = jnp.concatenate([coords, weights[None], thermal[None], jnp.zeros_like(coords)], axis=0)
    atoms = join(atoms, swap(atoms, "atom", 1))

    own_miller = lax.dynamic_slice_in_dim(miller[:, 0, :], j * own_count, own_count, 1)
    indices = own_miller.astype(jnp.float32)
    resolution = jnp.sum(indices * indices, axis=0) * (-LOG2E / (G * G))
    s2 = jnp.broadcast_to(resolution[:, None], (own_count, 128))
    lhs = indices.T[None, :, :, None] * jnp.eye(4, dtype=jnp.float32)[:, None, None, :]
    lhs = jnp.pad(lhs.reshape(4 * own_count, 12), ((0, 0), (0, 4)))
    lhs = jnp.concatenate([lhs, lhs, lhs], axis=1).astype(jnp.bfloat16)
    rc = jnp.pad(jnp.tile(angles.T, (3, 1)), ((0, 4), (0, 0)))
    y, core = j // 8, j % 2
    own = jnp.stack([core, g, j, y]).astype(jnp.int32)
    own = jnp.broadcast_to(own[:, None], (4, 128))
    indices, observed, own, atoms = lax.optimization_barrier((indices, observed[:, 0, :], own, atoms))

    acc, skip = None, 0
    for mask in (2, 8, 4, 16):
        more = swap(atoms, "atom", mask)
        acc = phase_call(lhs, s2, rc, [atoms], skip, acc, None, None, scales)
        if skip == 0:
            acc, rc = acc
        more, acc = lax.optimization_barrier((more, acc))
        if mask != 16:
            skip = atoms.shape[1]
            atoms = join(atoms, more)
    payload = phase_call(lhs, s2, rc, [more], 0, acc, observed, indices, scales)

    plane = lax.all_to_all(
        payload, ("atom", "refl"), 0, 0, tiled=True, axis_index_groups=plane_groups()
    )
    planes = [plane] + [swap(plane, "atom", 8 * step) for step in range(1, 4)]
    planes += [swap(plane, "atom", 1) for plane in planes]
    lines = [scatter_call(q // 4, q % 4, own, plane) for q, plane in enumerate(planes)]
    return transform_call(own, lines, first_table())


def solution(mesh):
    placed = (
        P(None, "atom"),
        P("atom"),
        P("atom"),
        P(),
        P(None, "refl", None),
        P(None, "refl", "atom"),
    )
    return jax.shard_map(
        shards, mesh=mesh, in_specs=placed, out_specs=P(None, "refl", "atom", None), check_vma=False
    )
```

```python
import functools
import math

import jax
import jax.numpy as jnp
import numpy as np
from jax import lax
from jax.experimental import pallas as pl
from jax.experimental.pallas import tpu as pltpu
from jax.sharding import PartitionSpec as P

G = 256
TILE = 256
LOG2E = math.log2(math.e)
PLANE = 32
ROWS = 11

SIN_C = (3.141592640183972, -5.167710090328514, 2.550077659663962, -0.5982921590533228, 0.07765940739590604)
COS_C = (0.9999999534665512, -4.934792858660287, 4.058411913867176, -1.3318801593277205, 0.21969679475921783)


def rotation_columns(angles):
    cosine, sine = jnp.cos(angles), jnp.sin(angles)
    cos_first, cos_tilt, cos_last = (cosine[:, q : q + 1] for q in range(3))
    sin_first, sin_tilt, sin_last = (sine[:, q : q + 1] for q in range(3))
    top_row = [
        cos_first * cos_tilt * cos_last - sin_first * sin_last,
        -cos_first * cos_tilt * sin_last - sin_first * cos_last,
        cos_first * sin_tilt,
    ]
    mid_row = [
        sin_first * cos_tilt * cos_last + cos_first * sin_last,
        -sin_first * cos_tilt * sin_last + cos_first * cos_last,
        sin_first * sin_tilt,
    ]
    low_row = [-sin_tilt * cos_last, sin_tilt * sin_last, cos_tilt]
    row = lax.broadcasted_iota(jnp.int32, (16, 1), 0)
    low_row = [jnp.where(row < 12, low, 0.0) for low in low_row]
    return [
        jnp.where(row < 4, top, jnp.where(row < 8, mid, low))
        for top, mid, low in zip(top_row, mid_row, low_row)
    ]


def monic(coefs):
    lead = coefs[-1]
    return lead, [c / lead for c in coefs[:-1]]


def horner_monic(u, rest):
    total = u + rest[-1]
    for c in rest[-2::-1]:
        total = total * u + c
    return total


def half_angle(t):
    t = t - jnp.round(t)
    u = t * t
    return t * horner_monic(u, SIN_M), horner_monic(u, COS_M)


SIN_K, SIN_M = monic(SIN_C)
COS_K, COS_M = monic(COS_C)


def sincos_turns(t):
    s, c = half_angle(t)
    return (2.0 * SIN_K * COS_K) * (s * c), 1.0 - (2.0 * SIN_K * SIN_K) * (s * s)


def split2(x):
    hi = x.astype(jnp.bfloat16)
    lo = (x - hi.astype(jnp.float32)).astype(jnp.bfloat16)
    return hi, lo


def phase_kernel(skip, first, last, *refs):
    lhs_ref, s2_ref, rc_ref, a_ref = refs[:4]
    pos = 4
    if not first:
        acc_in = refs[pos]
        pos += 1
    out_ref = refs[pos]
    pos += 1
    if rc_ref.shape[1] == 3:
        rc_out = refs[pos]
        pos += 1
        rc0, rc1, rc2 = rotation_columns(rc_ref[...])
        for q, column in enumerate((rc0, rc1, rc2)):
            rc_out[:, q : q + 1] = column
    else:
        rc0, rc1, rc2 = rc_ref[:, 0:1], rc_ref[:, 1:2], rc_ref[:, 2:3]
    if last:
        acc_ref = refs[pos]
        pos += 1
    else:
        acc_ref = out_ref
    even_ref, odd_ref = refs[pos : pos + 2]
    sets = lhs_ref.shape[0]

    if first:
        acc_ref[...] = jnp.zeros_like(acc_ref)
    else:
        acc_ref[...] = acc_in[...]

    def set_turns(n, i, turns_ref):
        a = a_ref[:, pl.ds(pl.multiple_of(i * TILE, TILE), TILE)]
        placed = rc0 * a[0:1] + rc1 * a[1:2] + rc2 * a[2:3]
        p1 = placed.astype(jnp.bfloat16)
        rest = placed - p1.astype(jnp.float32)
        p2 = rest.astype(jnp.bfloat16)
        p3 = (rest - p2.astype(jnp.float32)).astype(jnp.bfloat16)
        rhs = jnp.concatenate([p1, p2, p3], axis=0)
        turns_ref[...] = jnp.dot(lhs_ref[n], rhs, preferred_element_type=jnp.float32)

    def add_tile(n, i, turns_ref):
        a = a_ref[:, pl.ds(pl.multiple_of(i * TILE, TILE), TILE)]
        for nb in range(16):
            rows = slice(nb * 8, nb * 8 + 8)
            s2 = s2_ref[n, rows, :]
            amps = []
            for part in range(TILE // 128):
                lanes = slice(part * 128, part * 128 + 128)
                amps.append(a[3:4, lanes] * jnp.exp2(a[4:5, lanes] * s2))
            acc_ref[n, 8, rows, :] += sum(amps[1:], amps[0])
            for r in range(4):
                ms = mc = None
                for part in range(TILE // 128):
                    lanes = slice(part * 128, part * 128 + 128)
                    s, c = half_angle(turns_ref[r * 128 + nb * 8 : r * 128 + nb * 8 + 8, lanes])
                    m = amps[part] * s
                    ms = m * s if ms is None else ms + m * s
                    mc = m * c if mc is None else mc + m * c
                acc_ref[n, r, rows, :] += ms
                acc_ref[n, 4 + r, rows, :] += mc

    begin, tiles = skip // TILE, a_ref.shape[1] // TILE
    for n in range(sets):
        set_turns(n, begin, even_ref)

        @pl.loop(begin // 2, tiles // 2)
        def _(i):
            set_turns(n, 2 * i + 1, odd_ref)
            add_tile(n, 2 * i, even_ref)
            set_turns(n, jnp.minimum(2 * i + 2, tiles - 1), even_ref)
            add_tile(n, 2 * i + 1, odd_ref)

        if last:
            out_ref[n] = jnp.concatenate(
                [jnp.sum(acc_ref[n, q].T, axis=0, keepdims=True) for q in range(9)]
                + [jnp.zeros((7, 128), jnp.float32)],
                axis=0,
            )


def phase_call(lhs, s2, rc, atoms, skip, acc, last):
    first, sets, vmem = acc is None, lhs.shape[0], pl.BlockSpec(memory_space=pltpu.VMEM)
    operands = [lhs, s2, rc, atoms] + ([] if first else [acc])
    acc_shape = (sets, 9, 128, 128)
    scratch = [pltpu.VMEM((512, TILE), jnp.float32)] * 2
    if last:
        scratch = [pltpu.VMEM(acc_shape, jnp.float32)] + scratch
    out = [jax.ShapeDtypeStruct((sets, 16, 128) if last else acc_shape, jnp.float32)]
    if rc.shape[1] == 3:
        out.append(jax.ShapeDtypeStruct((16, 128), jnp.float32))
    count = (atoms.shape[1] - skip) * sets
    return pl.pallas_call(
        functools.partial(phase_kernel, skip, first, last),
        out_shape=out,
        in_specs=[vmem] * len(operands),
        out_specs=[vmem] * len(out),
        scratch_shapes=scratch,
        compiler_params=pltpu.CompilerParams(vmem_limit_bytes=16 << 20),
        cost_estimate=pl.CostEstimate(
            flops=count * 512 * 22, bytes_accessed=1 << 20, transcendentals=count * 128
        ),
        name="phases",
    )(*operands)


def coefficient_kernel(scales, own_ref, first_ref, second_ref, obs_ref, ind_ref, out_ref):
    atom_scale, refl_scale = scales
    sums = own_ref[0] + first_ref[0] + second_ref[0]
    obs0, obs1 = obs_ref[0:1, :], obs_ref[1:2, :]
    reals, imags = [], []
    for r in range(4):
        f_re = (sums[8:9] - (2.0 * SIN_K * SIN_K) * sums[r : r + 1]) * atom_scale
        f_im = ((2.0 * SIN_K * COS_K) * sums[4 + r : 5 + r]) * atom_scale
        reals.append((obs0 * f_re + obs1 * f_im) * refl_scale)
        imags.append((obs1 * f_re - obs0 * f_im) * refl_scale)
    for q, row in enumerate(reals + imags + [ind_ref[q : q + 1, :] for q in range(3)]):
        out_ref[:, q * 128 : q * 128 + 128] = jnp.broadcast_to(row, (PLANE, 128))


def coefficient_call(own, first, second, obs, indices, scales):
    vmem = pl.BlockSpec(memory_space=pltpu.VMEM)
    return pl.pallas_call(
        functools.partial(coefficient_kernel, scales),
        out_shape=jax.ShapeDtypeStruct((PLANE, ROWS * 128), jnp.float32),
        in_specs=[vmem] * 5,
        out_specs=vmem,
        compiler_params=pltpu.CompilerParams(vmem_limit_bytes=4 << 20),
        name="coefficients",
    )(own, first, second, obs, indices)


def scatter_kernel(other, step, own_ref, p_ref, x_ref):
    core, y, own_j = own_ref[0:1] ^ other, own_ref[3:4] ^ step, own_ref[2:3]
    cells = lax.broadcasted_iota(jnp.int32, (128, 128), 0).astype(jnp.float32)
    w_turn = (lax.broadcasted_iota(jnp.int32, (8, 128), 0) + own_j * 8).astype(
        jnp.float32
    ) * (1.0 / G)
    sub = lax.broadcasted_iota(jnp.int32, (8, 128), 0)
    for base in range(0, PLANE, 8):
        x = base // 8
        h = p_ref[base : base + 8, 8 * 128 : 9 * 128]
        k = p_ref[base : base + 8, 9 * 128 : 10 * 128]
        third = p_ref[base : base + 8, 10 * 128 : 11 * 128]
        h = jnp.where(h < 0.0, h + G, h) - (((sub >> 2) * 4 + x) * 32).astype(jnp.float32)
        k = jnp.where(k < 0.0, k + G, k) - (((y * 4 + (sub & 3)) * 2 + core) * 8).astype(jnp.float32)
        pair = jnp.floor(h * 0.5)
        odd = h - 2.0 * pair
        row = pair * 8.0 + k
        for q in range(8):
            i = base + q
            g, line = q // 4 * 4 + x, q % 4 * 8
            one_hot = jnp.where(cells == row[q : q + 1], 1.0, 0.0).astype(jnp.bfloat16)
            sine, cosine = sincos_turns(third[q : q + 1] * w_turn)
            reals, imags = [], []
            for r in range(4):
                re = p_ref[i : i + 1, r * 128 : r * 128 + 128]
                im = p_ref[i : i + 1, (4 + r) * 128 : (5 + r) * 128]
                reals.append(re * cosine - im * sine)
                imags.append(re * sine + im * cosine)
            hi, lo = split2(jnp.concatenate(reals + imags, axis=0))
            odd_row = jnp.broadcast_to(odd[q : q + 1], (32, 128)).astype(jnp.bfloat16)
            even_row = jnp.broadcast_to(1.0 - odd[q : q + 1], (32, 128)).astype(jnp.bfloat16)

            def masked(part):
                return jnp.concatenate(
                    [part[:32] * even_row, part[:32] * odd_row, part[32:] * even_row, part[32:] * odd_row],
                    axis=0,
                )

            total = lax.dot_general(
                jnp.concatenate([one_hot, one_hot], axis=1),
                jnp.concatenate([masked(hi), masked(lo)], axis=1),
                (((1,), (1,)), ((), ())),
                preferred_element_type=jnp.float32,
            )
            x_ref[g * 16 : g * 16 + 16, line : line + 8, :] = total.reshape(16, 8, 128)


def scatter_call(other, step, own, plane):
    vmem = pl.BlockSpec(memory_space=pltpu.VMEM)
    return pl.pallas_call(
        functools.partial(scatter_kernel, other, step),
        out_shape=jax.ShapeDtypeStruct((128, 32, 128), jnp.float32),
        in_specs=[vmem] * 2,
        out_specs=vmem,
        compiler_params=pltpu.CompilerParams(vmem_limit_bytes=16 << 20),
        cost_estimate=pl.CostEstimate(flops=1 << 29, bytes_accessed=1 << 20, transcendentals=0),
        name="scatter",
    )(own, plane)


def transform_kernel(own_ref, *refs):
    x_refs, (d_ref, out_ref, z_ref) = refs[:8], refs[8:]
    own_core, own_g, own_y = (jnp.concatenate([own_ref[q : q + 1]] * 2, axis=1) for q in (0, 1, 3))
    column = lax.broadcasted_iota(jnp.int32, (32, G), 1)
    y, core = own_y ^ ((column >> 5) & 3), own_core ^ (column >> 7)
    k = ((y * 4 + ((column >> 3) & 3)) * 2 + core) * 8 + (column & 7)
    v = lax.broadcasted_iota(jnp.int32, (32, G), 0) + own_g * 32
    sine, cosine = sincos_turns(((k * v) & (G - 1)).astype(jnp.float32) * (1.0 / G))
    table = jnp.concatenate(split2(jnp.concatenate([cosine, sine], axis=0)), axis=0)
    lane = lax.broadcasted_iota(jnp.int32, (32, 128), 1)
    sign = jnp.where(lane < 64, -1.0, 1.0)

    @pl.loop(0, 64, unroll=16)
    def _(i):
        sides = [jnp.concatenate([x_ref[2 * i + q] for x_ref in x_refs], axis=0) for q in range(2)]
        hi, lo = split2(jnp.concatenate(sides, axis=1))
        o1 = jnp.dot(table, hi, preferred_element_type=jnp.float32)
        o2 = jnp.dot(table[:64], lo, preferred_element_type=jnp.float32)
        z = o1[:64] + o1[64:] + o2
        for half in range(2):
            lanes = slice(half * 128, half * 128 + 128)
            combined = z[:32, lanes] + sign * pltpu.roll(z[32:, lanes], 64, 1)
            z_ref[pl.ds(2 * i + half, 32, stride=128), :] = combined

    @pl.loop(0, 4, unroll=4)
    def _(i):
        parts = []
        for q in range(8):
            zv = z_ref[pl.ds(pl.multiple_of((i * 8 + q) * 128, 128), 128), :].T
            parts.append(
                jnp.concatenate([zv[0:32], zv[32:64], zv[64:96], zv[96:128]], axis=1)
            )
        hi, lo = split2(jnp.concatenate(parts, axis=0))
        d_hi, d_lo = d_ref[0], d_ref[1]
        field = (
            jnp.dot(hi, d_hi, preferred_element_type=jnp.float32)
            + jnp.dot(lo, d_hi, preferred_element_type=jnp.float32)
            + jnp.dot(hi, d_lo, preferred_element_type=jnp.float32)
        )
        for q in range(8):
            for r in range(4):
                out_ref[r, i * 8 + q] = field[q * 32 + r * 8 : q * 32 + r * 8 + 8, :]


def split_np(x):
    hi = x.astype(np.float32).astype(jnp.bfloat16)
    lo = (x - hi.astype(np.float64)).astype(np.float32).astype(jnp.bfloat16)
    return hi, lo


def first_table():
    index = np.arange(G)
    angle = 2.0 * np.pi * ((index[:, None] * index[None, :]) % G) / G
    cos_hi, cos_lo = split_np(np.cos(angle))
    sin_hi, sin_lo = split_np(np.sin(angle))
    order = np.concatenate([np.arange(0, G, 2), np.arange(1, G, 2)])
    return np.stack(
        [
            np.concatenate([cos_hi[order], -sin_hi[order]]),
            np.concatenate([cos_lo[order], -sin_lo[order]]),
        ]
    )


def transform_call(own, pieces, first):
    vmem = pl.BlockSpec(memory_space=pltpu.VMEM)
    return pl.pallas_call(
        transform_kernel,
        out_shape=jax.ShapeDtypeStruct((4, 32, 8, G), jnp.float32),
        in_specs=[vmem] * 10,
        out_specs=vmem,
        scratch_shapes=[pltpu.VMEM((32 * 128, 128), jnp.float32)],
        compiler_params=pltpu.CompilerParams(vmem_limit_bytes=8 << 20),
        name="transform",
    )(own, *pieces, first)


def swap(x, axis, mask):
    count = lax.axis_size(axis)
    return lax.ppermute(x, axis, [(i, i ^ mask) for i in range(count)])


def flat(y, z, core, x):
    return ((y * 4 + z % 4) * 2 + core) * 8 + z // 4 * 4 + x


def plane_groups():
    return [
        [flat(y, z, core, x) for x in range(4) for z in range(8)] for y in range(4) for core in range(2)
    ]


def join_kernel(a_ref, b_ref, out_ref):
    size = a_ref.shape[1]
    out_ref[:, :size] = a_ref[...]
    out_ref[:, size:] = b_ref[...]


def join(a, b):
    vmem = pl.BlockSpec(memory_space=pltpu.VMEM)
    return pl.pallas_call(
        join_kernel,
        out_shape=jax.ShapeDtypeStruct((a.shape[0], 2 * a.shape[1]), jnp.float32),
        in_specs=[vmem, vmem],
        out_specs=vmem,
        compiler_params=pltpu.CompilerParams(vmem_limit_bytes=4 << 20),
        name="join",
    )(a, b)


def shards(coords, weights, thermal, angles, miller, observed):
    atom_count = lax.axis_size("atom")
    refl_count = lax.axis_size("refl")
    g = lax.axis_index("refl")
    j = lax.axis_index("atom")
    own_count = observed.shape[2]
    scales = (
        1.0 / math.sqrt(coords.shape[1] * atom_count),
        1.0 / math.sqrt(own_count * atom_count * refl_count),
    )
    atoms = jnp.concatenate([coords, weights[None], thermal[None], jnp.zeros_like(coords)], axis=0)
    atoms = join(atoms, swap(atoms, "atom", 1))

    sets = [
        lax.dynamic_slice_in_dim(miller[:, 0, :], (j ^ mask) * own_count, own_count, 1).astype(jnp.float32)
        for mask in (16, 20, 4, 0)
    ]
    indices = sets[3]
    sets = jnp.stack(sets)
    resolution = jnp.sum(sets * sets, axis=1) * (-LOG2E / (G * G))
    s2 = jnp.broadcast_to(resolution[:, :, None], (4, own_count, 128))
    lhs = jnp.transpose(sets, (0, 2, 1))[:, None, :, :, None] * jnp.eye(4, dtype=jnp.float32)[:, None, None, :]
    lhs = jnp.pad(lhs.reshape(4, 4 * own_count, 12), ((0, 0), (0, 0), (0, 4)))
    lhs = jnp.concatenate([lhs, lhs, lhs], axis=2).astype(jnp.bfloat16)
    rc = jnp.pad(jnp.tile(angles.T, (3, 1)), ((0, 4), (0, 0)))
    y, core = j // 8, j % 2
    own = jnp.stack([core, g, j, y]).astype(jnp.int32)
    own = jnp.broadcast_to(own[:, None], (4, 128))
    indices, observed, own, rc, atoms = lax.optimization_barrier(
        (indices, observed[:, 0, :], own, rc, atoms)
    )

    more = swap(atoms, "atom", 2)
    acc, rc = phase_call(lhs[:2], s2[:2], rc, atoms, 0, None, False)
    more, acc = lax.optimization_barrier((more, acc))
    atoms = join(atoms, more)
    more = swap(atoms, "atom", 8)
    (acc,) = phase_call(lhs[:2], s2[:2], rc, atoms, atoms.shape[1] // 2, acc, False)
    more, acc = lax.optimization_barrier((more, acc))
    atoms = join(atoms, more)
    (away,) = phase_call(lhs[:2], s2[:2], rc, atoms, atoms.shape[1] // 2, acc, True)
    near = swap(away, "atom", 16)
    (side,) = phase_call(lhs[2:3], s2[2:3], rc, atoms, 0, None, True)
    near, side = lax.optimization_barrier((near, side))
    across = swap(side + near[1:], "atom", 4)
    (here,) = phase_call(lhs[3:], s2[3:], rc, atoms, 0, None, True)
    across, here = lax.optimization_barrier((across, here))
    payload = coefficient_call(here, near, across, observed, indices, scales)

    plane = lax.all_to_all(
        payload, ("atom", "refl"), 0, 0, tiled=True, axis_index_groups=plane_groups()
    )
    planes = [plane] + [swap(plane, "atom", 8 * step) for step in range(1, 4)]
    planes += [swap(plane, "atom", 1) for plane in planes]
    lines = [scatter_call(q // 4, q % 4, own, plane) for q, plane in enumerate(planes)]
    return transform_call(own, lines, first_table())


def solution(mesh):
    placed = (
        P(None, "atom"),
        P("atom"),
        P("atom"),
        P(),
        P(None, "refl", None),
        P(None, "refl", "atom"),
    )
    return jax.shard_map(
        shards, mesh=mesh, in_specs=placed, out_specs=P(None, "refl", "atom", None), check_vma=False
    )
```

```python
import functools
import math

import jax
import jax.numpy as jnp
import numpy as np
from jax import lax
from jax.experimental import pallas as pl
from jax.experimental.pallas import tpu as pltpu
from jax.sharding import PartitionSpec as P

G = 256
TILE = 256
LOG2E = math.log2(math.e)
PLANE = 32
ROWS = 11

SIN_C = (3.141592640183972, -5.167710090328514, 2.550077659663962, -0.5982921590533228, 0.07765940739590604)
COS_C = (0.9999999534665512, -4.934792858660287, 4.058411913867176, -1.3318801593277205, 0.21969679475921783)


def rotation_columns(angles):
    cosine, sine = jnp.cos(angles), jnp.sin(angles)
    cos_first, cos_tilt, cos_last = (cosine[:, q : q + 1] for q in range(3))
    sin_first, sin_tilt, sin_last = (sine[:, q : q + 1] for q in range(3))
    top_row = [
        cos_first * cos_tilt * cos_last - sin_first * sin_last,
        -cos_first * cos_tilt * sin_last - sin_first * cos_last,
        cos_first * sin_tilt,
    ]
    mid_row = [
        sin_first * cos_tilt * cos_last + cos_first * sin_last,
        -sin_first * cos_tilt * sin_last + cos_first * cos_last,
        sin_first * sin_tilt,
    ]
    low_row = [-sin_tilt * cos_last, sin_tilt * sin_last, cos_tilt]
    row = lax.broadcasted_iota(jnp.int32, (16, 1), 0)
    low_row = [jnp.where(row < 12, low, 0.0) for low in low_row]
    return [
        jnp.where(row < 4, top, jnp.where(row < 8, mid, low))
        for top, mid, low in zip(top_row, mid_row, low_row)
    ]


def monic(coefs):
    lead = coefs[-1]
    return lead, [c / lead for c in coefs[:-1]]


def horner_monic(u, rest):
    total = u + rest[-1]
    for c in rest[-2::-1]:
        total = total * u + c
    return total


def half_angle(t):
    t = t - jnp.round(t)
    u = t * t
    return t * horner_monic(u, SIN_M), horner_monic(u, COS_M)


SIN_K, SIN_M = monic(SIN_C)
COS_K, COS_M = monic(COS_C)


def sincos_turns(t):
    s, c = half_angle(t)
    return (2.0 * SIN_K * COS_K) * (s * c), 1.0 - (2.0 * SIN_K * SIN_K) * (s * s)


def split2(x):
    hi = x.astype(jnp.bfloat16)
    lo = (x - hi.astype(jnp.float32)).astype(jnp.bfloat16)
    return hi, lo


def phase_kernel(tile, skip, first, last, *refs):
    lhs_ref, s2_ref, rc_ref, a_ref = refs[:4]
    pos = 4
    if not first:
        acc_in = refs[pos]
        pos += 1
    out_ref = refs[pos]
    pos += 1
    if rc_ref.shape[1] == 3:
        rc_out = refs[pos]
        pos += 1
        rc0, rc1, rc2 = rotation_columns(rc_ref[...])
        for q, column in enumerate((rc0, rc1, rc2)):
            rc_out[:, q : q + 1] = column
    else:
        rc0, rc1, rc2 = rc_ref[:, 0:1], rc_ref[:, 1:2], rc_ref[:, 2:3]
    if last:
        acc_ref = refs[pos]
        pos += 1
    else:
        acc_ref = out_ref
    even_ref, odd_ref = refs[pos : pos + 2]
    sets = lhs_ref.shape[0]

    if first:
        acc_ref[...] = jnp.zeros_like(acc_ref)
    else:
        acc_ref[...] = acc_in[...]

    def set_turns(n, i, turns_ref):
        a = a_ref[:, pl.ds(pl.multiple_of(i * tile, tile), tile)]
        placed = rc0 * a[0:1] + rc1 * a[1:2] + rc2 * a[2:3]
        p1 = placed.astype(jnp.bfloat16)
        rest = placed - p1.astype(jnp.float32)
        p2 = rest.astype(jnp.bfloat16)
        p3 = (rest - p2.astype(jnp.float32)).astype(jnp.bfloat16)
        rhs = jnp.concatenate([p1, p2, p3], axis=0)
        turns_ref[...] = jnp.dot(lhs_ref[n], rhs, preferred_element_type=jnp.float32)

    def add_tile(n, i, turns_ref):
        a = a_ref[:, pl.ds(pl.multiple_of(i * tile, tile), tile)]
        for nb in range(16):
            rows = slice(nb * 8, nb * 8 + 8)
            s2 = s2_ref[n, rows, :]
            amps = []
            for part in range(tile // 128):
                lanes = slice(part * 128, part * 128 + 128)
                amps.append(a[3:4, lanes] * jnp.exp2(a[4:5, lanes] * s2))
            acc_ref[n, 8, rows, :] += sum(amps[1:], amps[0])
            for r in range(4):
                ms = mc = None
                for part in range(tile // 128):
                    lanes = slice(part * 128, part * 128 + 128)
                    s, c = half_angle(turns_ref[r * 128 + nb * 8 : r * 128 + nb * 8 + 8, lanes])
                    m = amps[part] * s
                    ms = m * s if ms is None else ms + m * s
                    mc = m * c if mc is None else mc + m * c
                acc_ref[n, r, rows, :] += ms
                acc_ref[n, 4 + r, rows, :] += mc

    begin, tiles = skip // tile, a_ref.shape[1] // tile
    for n in range(sets):
        set_turns(n, begin, even_ref)

        @pl.loop(begin // 2, tiles // 2)
        def _(i):
            set_turns(n, 2 * i + 1, odd_ref)
            add_tile(n, 2 * i, even_ref)
            set_turns(n, jnp.minimum(2 * i + 2, tiles - 1), even_ref)
            add_tile(n, 2 * i + 1, odd_ref)

        if last:
            out_ref[n] = jnp.concatenate(
                [jnp.sum(acc_ref[n, q].T, axis=0, keepdims=True) for q in range(9)]
                + [jnp.zeros((7, 128), jnp.float32)],
                axis=0,
            )


def phase_call(lhs, s2, rc, atoms, skip, acc, last):
    first, sets, vmem = acc is None, lhs.shape[0], pl.BlockSpec(memory_space=pltpu.VMEM)
    operands = [lhs, s2, rc, atoms] + ([] if first else [acc])
    acc_shape = (sets, 9, 128, 128)
    tile = TILE if skip % (2 * TILE) or (atoms.shape[1] - skip) % (2 * TILE) else 2 * TILE
    tile = TILE if atoms.shape[1] - skip < 4 * TILE or skip % (4 * TILE) else tile
    scratch = [pltpu.VMEM((512, tile), jnp.float32)] * 2
    if last:
        scratch = [pltpu.VMEM(acc_shape, jnp.float32)] + scratch
    out = [jax.ShapeDtypeStruct((sets, 16, 128) if last else acc_shape, jnp.float32)]
    if rc.shape[1] == 3:
        out.append(jax.ShapeDtypeStruct((16, 128), jnp.float32))
    count = (atoms.shape[1] - skip) * sets
    return pl.pallas_call(
        functools.partial(phase_kernel, tile, skip, first, last),
        out_shape=out,
        in_specs=[vmem] * len(operands),
        out_specs=[vmem] * len(out),
        scratch_shapes=scratch,
        compiler_params=pltpu.CompilerParams(vmem_limit_bytes=16 << 20),
        cost_estimate=pl.CostEstimate(
            flops=count * 512 * 22, bytes_accessed=1 << 20, transcendentals=count * 128
        ),
        name="phases",
    )(*operands)


def coefficient_kernel(scales, own_ref, first_ref, second_ref, obs_ref, ind_ref, out_ref):
    atom_scale, refl_scale = scales
    sums = own_ref[0] + first_ref[0] + second_ref[0]
    obs0, obs1 = obs_ref[0:1, :], obs_ref[1:2, :]
    reals, imags = [], []
    for r in range(4):
        f_re = (sums[8:9] - (2.0 * SIN_K * SIN_K) * sums[r : r + 1]) * atom_scale
        f_im = ((2.0 * SIN_K * COS_K) * sums[4 + r : 5 + r]) * atom_scale
        reals.append((obs0 * f_re + obs1 * f_im) * refl_scale)
        imags.append((obs1 * f_re - obs0 * f_im) * refl_scale)
    for q, row in enumerate(reals + imags + [ind_ref[q : q + 1, :] for q in range(3)]):
        out_ref[:, q * 128 : q * 128 + 128] = jnp.broadcast_to(row, (PLANE, 128))


def coefficient_call(own, first, second, obs, indices, scales):
    vmem = pl.BlockSpec(memory_space=pltpu.VMEM)
    return pl.pallas_call(
        functools.partial(coefficient_kernel, scales),
        out_shape=jax.ShapeDtypeStruct((PLANE, ROWS * 128), jnp.float32),
        in_specs=[vmem] * 5,
        out_specs=vmem,
        compiler_params=pltpu.CompilerParams(vmem_limit_bytes=4 << 20),
        name="coefficients",
    )(own, first, second, obs, indices)


def scatter_kernel(other, step, own_ref, p_ref, x_ref):
    core, y, own_j = own_ref[0:1] ^ other, own_ref[3:4] ^ step, own_ref[2:3]
    cells = lax.broadcasted_iota(jnp.int32, (128, 128), 0).astype(jnp.float32)
    w_turn = (lax.broadcasted_iota(jnp.int32, (8, 128), 0) + own_j * 8).astype(
        jnp.float32
    ) * (1.0 / G)
    sub = lax.broadcasted_iota(jnp.int32, (8, 128), 0)
    for base in range(0, PLANE, 8):
        x = base // 8
        h = p_ref[base : base + 8, 8 * 128 : 9 * 128]
        k = p_ref[base : base + 8, 9 * 128 : 10 * 128]
        third = p_ref[base : base + 8, 10 * 128 : 11 * 128]
        h = jnp.where(h < 0.0, h + G, h) - (((sub >> 2) * 4 + x) * 32).astype(jnp.float32)
        k = jnp.where(k < 0.0, k + G, k) - (((y * 4 + (sub & 3)) * 2 + core) * 8).astype(jnp.float32)
        pair = jnp.floor(h * 0.5)
        odd = h - 2.0 * pair
        row = pair * 8.0 + k
        for q in range(8):
            i = base + q
            g, line = q // 4 * 4 + x, q % 4 * 8
            one_hot = jnp.where(cells == row[q : q + 1], 1.0, 0.0).astype(jnp.bfloat16)
            sine, cosine = sincos_turns(third[q : q + 1] * w_turn)
            reals, imags = [], []
            for r in range(4):
                re = p_ref[i : i + 1, r * 128 : r * 128 + 128]
                im = p_ref[i : i + 1, (4 + r) * 128 : (5 + r) * 128]
                reals.append(re * cosine - im * sine)
                imags.append(re * sine + im * cosine)
            hi, lo = split2(jnp.concatenate(reals + imags, axis=0))
            odd_row = jnp.broadcast_to(odd[q : q + 1], (32, 128)).astype(jnp.bfloat16)
            even_row = jnp.broadcast_to(1.0 - odd[q : q + 1], (32, 128)).astype(jnp.bfloat16)

            def masked(part):
                return jnp.concatenate(
                    [part[:32] * even_row, part[:32] * odd_row, part[32:] * even_row, part[32:] * odd_row],
                    axis=0,
                )

            total = lax.dot_general(
                jnp.concatenate([one_hot, one_hot], axis=1),
                jnp.concatenate([masked(hi), masked(lo)], axis=1),
                (((1,), (1,)), ((), ())),
                preferred_element_type=jnp.float32,
            )
            x_ref[g * 16 : g * 16 + 16, line : line + 8, :] = total.reshape(16, 8, 128)


def scatter_call(other, step, own, plane):
    vmem = pl.BlockSpec(memory_space=pltpu.VMEM)
    return pl.pallas_call(
        functools.partial(scatter_kernel, other, step),
        out_shape=jax.ShapeDtypeStruct((128, 32, 128), jnp.float32),
        in_specs=[vmem] * 2,
        out_specs=vmem,
        compiler_params=pltpu.CompilerParams(vmem_limit_bytes=16 << 20),
        cost_estimate=pl.CostEstimate(flops=1 << 29, bytes_accessed=1 << 20, transcendentals=0),
        name="scatter",
    )(own, plane)


def transform_kernel(own_ref, *refs):
    x_refs, (d_ref, out_ref, z_ref) = refs[:8], refs[8:]
    own_core, own_g, own_y = (jnp.concatenate([own_ref[q : q + 1]] * 2, axis=1) for q in (0, 1, 3))
    column = lax.broadcasted_iota(jnp.int32, (32, G), 1)
    y, core = own_y ^ ((column >> 5) & 3), own_core ^ (column >> 7)
    k = ((y * 4 + ((column >> 3) & 3)) * 2 + core) * 8 + (column & 7)
    v = lax.broadcasted_iota(jnp.int32, (32, G), 0) + own_g * 32
    sine, cosine = sincos_turns(((k * v) & (G - 1)).astype(jnp.float32) * (1.0 / G))
    table = jnp.concatenate(split2(jnp.concatenate([cosine, sine], axis=0)), axis=0)
    lane = lax.broadcasted_iota(jnp.int32, (32, 128), 1)
    sign = jnp.where(lane < 64, -1.0, 1.0)

    @pl.loop(0, 64, unroll=16)
    def _(i):
        sides = [jnp.concatenate([x_ref[2 * i + q] for x_ref in x_refs], axis=0) for q in range(2)]
        hi, lo = split2(jnp.concatenate(sides, axis=1))
        o1 = jnp.dot(table, hi, preferred_element_type=jnp.float32)
        o2 = jnp.dot(table[:64], lo, preferred_element_type=jnp.float32)
        z = o1[:64] + o1[64:] + o2
        for half in range(2):
            lanes = slice(half * 128, half * 128 + 128)
            combined = z[:32, lanes] + sign * pltpu.roll(z[32:, lanes], 64, 1)
            z_ref[pl.ds(2 * i + half, 32, stride=128), :] = combined

    @pl.loop(0, 4, unroll=4)
    def _(i):
        parts = []
        for q in range(8):
            zv = z_ref[pl.ds(pl.multiple_of((i * 8 + q) * 128, 128), 128), :].T
            parts.append(
                jnp.concatenate([zv[0:32], zv[32:64], zv[64:96], zv[96:128]], axis=1)
            )
        hi, lo = split2(jnp.concatenate(parts, axis=0))
        d_hi, d_lo = d_ref[0], d_ref[1]
        field = (
            jnp.dot(hi, d_hi, preferred_element_type=jnp.float32)
            + jnp.dot(lo, d_hi, preferred_element_type=jnp.float32)
            + jnp.dot(hi, d_lo, preferred_element_type=jnp.float32)
        )
        for q in range(8):
            for r in range(4):
                out_ref[r, i * 8 + q] = field[q * 32 + r * 8 : q * 32 + r * 8 + 8, :]


def split_np(x):
    hi = x.astype(np.float32).astype(jnp.bfloat16)
    lo = (x - hi.astype(np.float64)).astype(np.float32).astype(jnp.bfloat16)
    return hi, lo


def first_table():
    index = np.arange(G)
    angle = 2.0 * np.pi * ((index[:, None] * index[None, :]) % G) / G
    cos_hi, cos_lo = split_np(np.cos(angle))
    sin_hi, sin_lo = split_np(np.sin(angle))
    order = np.concatenate([np.arange(0, G, 2), np.arange(1, G, 2)])
    return np.stack(
        [
            np.concatenate([cos_hi[order], -sin_hi[order]]),
            np.concatenate([cos_lo[order], -sin_lo[order]]),
        ]
    )


def transform_call(own, pieces, first):
    vmem = pl.BlockSpec(memory_space=pltpu.VMEM)
    return pl.pallas_call(
        transform_kernel,
        out_shape=jax.ShapeDtypeStruct((4, 32, 8, G), jnp.float32),
        in_specs=[vmem] * 10,
        out_specs=vmem,
        scratch_shapes=[pltpu.VMEM((32 * 128, 128), jnp.float32)],
        compiler_params=pltpu.CompilerParams(vmem_limit_bytes=8 << 20),
        name="transform",
    )(own, *pieces, first)


def swap(x, axis, mask):
    count = lax.axis_size(axis)
    return lax.ppermute(x, axis, [(i, i ^ mask) for i in range(count)])


def flat(y, z, core, x):
    return ((y * 4 + z % 4) * 2 + core) * 8 + z // 4 * 4 + x


def plane_groups():
    return [
        [flat(y, z, core, x) for x in range(4) for z in range(8)] for y in range(4) for core in range(2)
    ]


def join_kernel(a_ref, b_ref, out_ref):
    size = a_ref.shape[1]
    out_ref[:, :size] = a_ref[...]
    out_ref[:, size:] = b_ref[...]


def join(a, b):
    vmem = pl.BlockSpec(memory_space=pltpu.VMEM)
    return pl.pallas_call(
        join_kernel,
        out_shape=jax.ShapeDtypeStruct((a.shape[0], 2 * a.shape[1]), jnp.float32),
        in_specs=[vmem, vmem],
        out_specs=vmem,
        compiler_params=pltpu.CompilerParams(vmem_limit_bytes=4 << 20),
        name="join",
    )(a, b)


def shards(coords, weights, thermal, angles, miller, observed):
    atom_count = lax.axis_size("atom")
    refl_count = lax.axis_size("refl")
    g = lax.axis_index("refl")
    j = lax.axis_index("atom")
    own_count = observed.shape[2]
    scales = (
        1.0 / math.sqrt(coords.shape[1] * atom_count),
        1.0 / math.sqrt(own_count * atom_count * refl_count),
    )
    atoms = jnp.concatenate([coords, weights[None], thermal[None], jnp.zeros_like(coords)], axis=0)
    atoms = join(atoms, swap(atoms, "atom", 1))

    sets = [
        lax.dynamic_slice_in_dim(miller[:, 0, :], (j ^ mask) * own_count, own_count, 1).astype(jnp.float32)
        for mask in (16, 20, 4, 0)
    ]
    indices = sets[3]
    sets = jnp.stack(sets)
    resolution = jnp.sum(sets * sets, axis=1) * (-LOG2E / (G * G))
    s2 = jnp.broadcast_to(resolution[:, :, None], (4, own_count, 128))
    lhs = jnp.transpose(sets, (0, 2, 1))[:, None, :, :, None] * jnp.eye(4, dtype=jnp.float32)[:, None, None, :]
    lhs = jnp.pad(lhs.reshape(4, 4 * own_count, 12), ((0, 0), (0, 0), (0, 4)))
    lhs = jnp.concatenate([lhs, lhs, lhs], axis=2).astype(jnp.bfloat16)
    rc = jnp.pad(jnp.tile(angles.T, (3, 1)), ((0, 4), (0, 0)))
    y, core = j // 8, j % 2
    own = jnp.stack([core, g, j, y]).astype(jnp.int32)
    own = jnp.broadcast_to(own[:, None], (4, 128))
    indices, observed, own, rc, atoms = lax.optimization_barrier(
        (indices, observed[:, 0, :], own, rc, atoms)
    )

    more = swap(atoms, "atom", 2)
    acc, rc = phase_call(lhs[:2], s2[:2], rc, atoms, 0, None, False)
    more, acc = lax.optimization_barrier((more, acc))
    atoms = join(atoms, more)
    more = swap(atoms, "atom", 8)
    (acc,) = phase_call(lhs[:2], s2[:2], rc, atoms, atoms.shape[1] // 2, acc, False)
    more, acc = lax.optimization_barrier((more, acc))
    atoms = join(atoms, more)
    (away,) = phase_call(lhs[:2], s2[:2], rc, atoms, atoms.shape[1] // 2, acc, True)
    near = swap(away, "atom", 16)
    (side,) = phase_call(lhs[2:3], s2[2:3], rc, atoms, 0, None, True)
    near, side = lax.optimization_barrier((near, side))
    across = swap(side + near[1:], "atom", 4)
    (here,) = phase_call(lhs[3:], s2[3:], rc, atoms, 0, None, True)
    across, here = lax.optimization_barrier((across, here))
    payload = coefficient_call(here, near, across, observed, indices, scales)

    plane = lax.all_to_all(
        payload, ("atom", "refl"), 0, 0, tiled=True, axis_index_groups=plane_groups()
    )
    planes = [plane] + [swap(plane, "atom", 8 * step) for step in range(1, 4)]
    planes += [swap(plane, "atom", 1) for plane in planes]
    lines = [scatter_call(q // 4, q % 4, own, plane) for q, plane in enumerate(planes)]
    return transform_call(own, lines, first_table())


def solution(mesh):
    placed = (
        P(None, "atom"),
        P("atom"),
        P("atom"),
        P(),
        P(None, "refl", None),
        P(None, "refl", "atom"),
    )
    return jax.shard_map(
        shards, mesh=mesh, in_specs=placed, out_specs=P(None, "refl", "atom", None), check_vma=False
    )
```

```python
import functools
import math

import jax
import jax.numpy as jnp
import numpy as np
from jax import lax
from jax.experimental import pallas as pl
from jax.experimental.pallas import tpu as pltpu
from jax.sharding import PartitionSpec as P

G = 256
TILE = 256
LOG2E = math.log2(math.e)
PLANE = 32
ROWS = 11

SIN_C = (3.141592640183972, -5.167710090328514, 2.550077659663962, -0.5982921590533228, 0.07765940739590604)
COS_C = (0.9999999534665512, -4.934792858660287, 4.058411913867176, -1.3318801593277205, 0.21969679475921783)


def rotation_columns(angles):
    cosine, sine = jnp.cos(angles), jnp.sin(angles)
    cos_first, cos_tilt, cos_last = (cosine[:, q : q + 1] for q in range(3))
    sin_first, sin_tilt, sin_last = (sine[:, q : q + 1] for q in range(3))
    top_row = [
        cos_first * cos_tilt * cos_last - sin_first * sin_last,
        -cos_first * cos_tilt * sin_last - sin_first * cos_last,
        cos_first * sin_tilt,
    ]
    mid_row = [
        sin_first * cos_tilt * cos_last + cos_first * sin_last,
        -sin_first * cos_tilt * sin_last + cos_first * cos_last,
        sin_first * sin_tilt,
    ]
    low_row = [-sin_tilt * cos_last, sin_tilt * sin_last, cos_tilt]
    row = lax.broadcasted_iota(jnp.int32, (16, 1), 0)
    low_row = [jnp.where(row < 12, low, 0.0) for low in low_row]
    return [
        jnp.where(row < 4, top, jnp.where(row < 8, mid, low))
        for top, mid, low in zip(top_row, mid_row, low_row)
    ]


def monic(coefs):
    lead = coefs[-1]
    return lead, [c / lead for c in coefs[:-1]]


def horner_monic(u, rest):
    total = u + rest[-1]
    for c in rest[-2::-1]:
        total = total * u + c
    return total


def half_angle(t):
    t = t - jnp.round(t)
    u = t * t
    return t * horner_monic(u, SIN_M), horner_monic(u, COS_M)


SIN_K, SIN_M = monic(SIN_C)
COS_K, COS_M = monic(COS_C)


def sincos_turns(t):
    s, c = half_angle(t)
    return (2.0 * SIN_K * COS_K) * (s * c), 1.0 - (2.0 * SIN_K * SIN_K) * (s * s)


def split2(x):
    hi = x.astype(jnp.bfloat16)
    lo = (x - hi.astype(jnp.float32)).astype(jnp.bfloat16)
    return hi, lo


def phase_kernel(tile, skip, first, last, *refs):
    lhs_ref, s2_ref, rc_ref, a_ref = refs[:4]
    pos = 4
    if not first:
        acc_in = refs[pos]
        pos += 1
    out_ref = refs[pos]
    pos += 1
    if rc_ref.shape[1] == 3:
        rc_out = refs[pos]
        pos += 1
        rc0, rc1, rc2 = rotation_columns(rc_ref[...])
        for q, column in enumerate((rc0, rc1, rc2)):
            rc_out[:, q : q + 1] = column
    else:
        rc0, rc1, rc2 = rc_ref[:, 0:1], rc_ref[:, 1:2], rc_ref[:, 2:3]
    if last:
        acc_ref = refs[pos]
        pos += 1
    else:
        acc_ref = out_ref
    even_ref, odd_ref = refs[pos : pos + 2]
    sets = lhs_ref.shape[0]

    if first:
        acc_ref[...] = jnp.zeros_like(acc_ref)
    else:
        acc_ref[...] = acc_in[...]

    def set_turns(n, i, turns_ref):
        a = a_ref[:, pl.ds(pl.multiple_of(i * tile, tile), tile)]
        placed = rc0 * a[0:1] + rc1 * a[1:2] + rc2 * a[2:3]
        p1 = placed.astype(jnp.bfloat16)
        rest = placed - p1.astype(jnp.float32)
        p2 = rest.astype(jnp.bfloat16)
        p3 = (rest - p2.astype(jnp.float32)).astype(jnp.bfloat16)
        rhs = jnp.concatenate([p1, p2, p3], axis=0)
        turns_ref[...] = jnp.dot(lhs_ref[n], rhs, preferred_element_type=jnp.float32)

    def add_tile(n, i, turns_ref):
        a = a_ref[:, pl.ds(pl.multiple_of(i * tile, tile), tile)]
        for nb in range(16):
            rows = slice(nb * 8, nb * 8 + 8)
            s2 = s2_ref[n, rows, :]
            amps = []
            for part in range(tile // 128):
                lanes = slice(part * 128, part * 128 + 128)
                amps.append(a[3:4, lanes] * jnp.exp2(a[4:5, lanes] * s2))
            acc_ref[n, 8, rows, :] += sum(amps[1:], amps[0])
            for r in range(4):
                ms = mc = None
                for part in range(tile // 128):
                    lanes = slice(part * 128, part * 128 + 128)
                    s, c = half_angle(turns_ref[r * 128 + nb * 8 : r * 128 + nb * 8 + 8, lanes])
                    m = amps[part] * s
                    ms = m * s if ms is None else ms + m * s
                    mc = m * c if mc is None else mc + m * c
                acc_ref[n, r, rows, :] += ms
                acc_ref[n, 4 + r, rows, :] += mc

    begin, tiles = skip // tile, a_ref.shape[1] // tile
    for n in range(sets):
        set_turns(n, begin, even_ref)

        @pl.loop(begin // 2, tiles // 2)
        def _(i):
            set_turns(n, 2 * i + 1, odd_ref)
            add_tile(n, 2 * i, even_ref)
            set_turns(n, jnp.minimum(2 * i + 2, tiles - 1), even_ref)
            add_tile(n, 2 * i + 1, odd_ref)

        if last:
            out_ref[n] = jnp.concatenate(
                [jnp.sum(acc_ref[n, q].T, axis=0, keepdims=True) for q in range(9)]
                + [jnp.zeros((7, 128), jnp.float32)],
                axis=0,
            )


def phase_call(lhs, s2, rc, atoms, skip, acc, last):
    first, sets, vmem = acc is None, lhs.shape[0], pl.BlockSpec(memory_space=pltpu.VMEM)
    operands = [lhs, s2, rc, atoms] + ([] if first else [acc])
    acc_shape = (sets, 9, 128, 128)
    tile = TILE if skip % (2 * TILE) or (atoms.shape[1] - skip) % (2 * TILE) else 2 * TILE
    tile = TILE if atoms.shape[1] - skip < 4 * TILE or skip % (4 * TILE) else tile
    scratch = [pltpu.VMEM((512, tile), jnp.float32)] * 2
    if last:
        scratch = [pltpu.VMEM(acc_shape, jnp.float32)] + scratch
    out = [jax.ShapeDtypeStruct((sets, 16, 128) if last else acc_shape, jnp.float32)]
    if rc.shape[1] == 3:
        out.append(jax.ShapeDtypeStruct((16, 128), jnp.float32))
    count = (atoms.shape[1] - skip) * sets
    return pl.pallas_call(
        functools.partial(phase_kernel, tile, skip, first, last),
        out_shape=out,
        in_specs=[vmem] * len(operands),
        out_specs=[vmem] * len(out),
        scratch_shapes=scratch,
        compiler_params=pltpu.CompilerParams(vmem_limit_bytes=16 << 20),
        cost_estimate=pl.CostEstimate(
            flops=count * 512 * 22, bytes_accessed=1 << 20, transcendentals=count * 128
        ),
        name="phases",
    )(*operands)


def coefficient_kernel(scales, own_ref, first_ref, second_ref, obs_ref, ind_ref, out_ref):
    atom_scale, refl_scale = scales
    sums = own_ref[0] + first_ref[0] + second_ref[0]
    obs0, obs1 = obs_ref[0:1, :], obs_ref[1:2, :]
    reals, imags = [], []
    for r in range(4):
        f_re = (sums[8:9] - (2.0 * SIN_K * SIN_K) * sums[r : r + 1]) * atom_scale
        f_im = ((2.0 * SIN_K * COS_K) * sums[4 + r : 5 + r]) * atom_scale
        reals.append((obs0 * f_re + obs1 * f_im) * refl_scale)
        imags.append((obs1 * f_re - obs0 * f_im) * refl_scale)
    for q, row in enumerate(reals + imags + [ind_ref[q : q + 1, :] for q in range(3)]):
        out_ref[:, q * 128 : q * 128 + 128] = jnp.broadcast_to(row, (PLANE, 128))


def coefficient_call(own, first, second, obs, indices, scales):
    vmem = pl.BlockSpec(memory_space=pltpu.VMEM)
    return pl.pallas_call(
        functools.partial(coefficient_kernel, scales),
        out_shape=jax.ShapeDtypeStruct((PLANE, ROWS * 128), jnp.float32),
        in_specs=[vmem] * 5,
        out_specs=vmem,
        compiler_params=pltpu.CompilerParams(vmem_limit_bytes=4 << 20),
        name="coefficients",
    )(own, first, second, obs, indices)


def scatter_kernel(other, step, own_ref, p_ref, x_ref):
    core, y, own_j = own_ref[0:1] ^ other, own_ref[3:4] ^ step, own_ref[2:3]
    cells = lax.broadcasted_iota(jnp.int32, (128, 128), 0).astype(jnp.float32)
    w_turn = (lax.broadcasted_iota(jnp.int32, (8, 128), 0) + own_j * 8).astype(
        jnp.float32
    ) * (1.0 / G)
    sub = lax.broadcasted_iota(jnp.int32, (8, 128), 0)
    for base in range(0, PLANE, 8):
        x = base // 8
        h = p_ref[base : base + 8, 8 * 128 : 9 * 128]
        k = p_ref[base : base + 8, 9 * 128 : 10 * 128]
        third = p_ref[base : base + 8, 10 * 128 : 11 * 128]
        h = jnp.where(h < 0.0, h + G, h) - (((sub >> 2) * 4 + x) * 32).astype(jnp.float32)
        k = jnp.where(k < 0.0, k + G, k) - (((y * 4 + (sub & 3)) * 2 + core) * 8).astype(jnp.float32)
        pair = jnp.floor(h * 0.5)
        odd = h - 2.0 * pair
        row = pair * 8.0 + k
        for q in range(8):
            i = base + q
            g, line = q // 4 * 4 + x, q % 4 * 8
            one_hot = jnp.where(cells == row[q : q + 1], 1.0, 0.0).astype(jnp.bfloat16)
            sine, cosine = sincos_turns(third[q : q + 1] * w_turn)
            reals, imags = [], []
            for r in range(4):
                re = p_ref[i : i + 1, r * 128 : r * 128 + 128]
                im = p_ref[i : i + 1, (4 + r) * 128 : (5 + r) * 128]
                reals.append(re * cosine - im * sine)
                imags.append(re * sine + im * cosine)
            hi, lo = split2(jnp.concatenate(reals + imags, axis=0))
            odd_row = jnp.broadcast_to(odd[q : q + 1], (32, 128)).astype(jnp.bfloat16)
            even_row = jnp.broadcast_to(1.0 - odd[q : q + 1], (32, 128)).astype(jnp.bfloat16)

            def masked(part):
                return jnp.concatenate(
                    [part[:32] * even_row, part[:32] * odd_row, part[32:] * even_row, part[32:] * odd_row],
                    axis=0,
                )

            total = lax.dot_general(
                jnp.concatenate([one_hot, one_hot], axis=1),
                jnp.concatenate([masked(hi), masked(lo)], axis=1),
                (((1,), (1,)), ((), ())),
                preferred_element_type=jnp.float32,
            )
            x_ref[g * 16 : g * 16 + 16, line : line + 8, :] = total.reshape(16, 8, 128)


def scatter_call(other, step, own, plane):
    vmem = pl.BlockSpec(memory_space=pltpu.VMEM)
    return pl.pallas_call(
        functools.partial(scatter_kernel, other, step),
        out_shape=jax.ShapeDtypeStruct((128, 32, 128), jnp.float32),
        in_specs=[vmem] * 2,
        out_specs=vmem,
        compiler_params=pltpu.CompilerParams(vmem_limit_bytes=16 << 20),
        cost_estimate=pl.CostEstimate(flops=1 << 29, bytes_accessed=1 << 20, transcendentals=0),
        name="scatter",
    )(own, plane)


def transform_kernel(own_ref, *refs):
    x_refs, (d_ref, out_ref, z_ref, field_ref, sems) = refs[:8], refs[8:]
    own_core, own_g, own_y = (jnp.concatenate([own_ref[q : q + 1]] * 2, axis=1) for q in (0, 1, 3))
    column = lax.broadcasted_iota(jnp.int32, (32, G), 1)
    y, core = own_y ^ ((column >> 5) & 3), own_core ^ (column >> 7)
    k = ((y * 4 + ((column >> 3) & 3)) * 2 + core) * 8 + (column & 7)
    v = lax.broadcasted_iota(jnp.int32, (32, G), 0) + own_g * 32
    sine, cosine = sincos_turns(((k * v) & (G - 1)).astype(jnp.float32) * (1.0 / G))
    table = jnp.concatenate(split2(jnp.concatenate([cosine, sine], axis=0)), axis=0)
    lane = lax.broadcasted_iota(jnp.int32, (32, 128), 1)
    sign = jnp.where(lane < 64, -1.0, 1.0)

    @pl.loop(0, 64, unroll=16)
    def _(i):
        sides = [jnp.concatenate([x_ref[2 * i + q] for x_ref in x_refs], axis=0) for q in range(2)]
        hi, lo = split2(jnp.concatenate(sides, axis=1))
        o1 = jnp.dot(table, hi, preferred_element_type=jnp.float32)
        o2 = jnp.dot(table[:64], lo, preferred_element_type=jnp.float32)
        z = o1[:64] + o1[64:] + o2
        for half in range(2):
            lanes = slice(half * 128, half * 128 + 128)
            combined = z[:32, lanes] + sign * pltpu.roll(z[32:, lanes], 64, 1)
            z_ref[pl.ds(2 * i + half, 32, stride=128), :] = combined

    copies = []
    for i in range(4):
        parts = []
        for q in range(8):
            zv = z_ref[(i * 8 + q) * 128 : (i * 8 + q + 1) * 128, :].T
            parts.append(
                jnp.concatenate([zv[0:32], zv[32:64], zv[64:96], zv[96:128]], axis=1)
            )
        hi, lo = split2(jnp.concatenate(parts, axis=0))
        d_hi, d_lo = d_ref[0], d_ref[1]
        field = (
            jnp.dot(hi, d_hi, preferred_element_type=jnp.float32)
            + jnp.dot(lo, d_hi, preferred_element_type=jnp.float32)
            + jnp.dot(hi, d_lo, preferred_element_type=jnp.float32)
        )
        for q in range(8):
            for r in range(4):
                field_ref[i, r, q] = field[q * 32 + r * 8 : q * 32 + r * 8 + 8, :]
        copies.append(
            pltpu.make_async_copy(field_ref.at[i], out_ref.at[:, i * 8 : i * 8 + 8], sems.at[i])
        )
        copies[-1].start()
    for copy in copies:
        copy.wait()


def split_np(x):
    hi = x.astype(np.float32).astype(jnp.bfloat16)
    lo = (x - hi.astype(np.float64)).astype(np.float32).astype(jnp.bfloat16)
    return hi, lo


def first_table():
    index = np.arange(G)
    angle = 2.0 * np.pi * ((index[:, None] * index[None, :]) % G) / G
    cos_hi, cos_lo = split_np(np.cos(angle))
    sin_hi, sin_lo = split_np(np.sin(angle))
    order = np.concatenate([np.arange(0, G, 2), np.arange(1, G, 2)])
    return np.stack(
        [
            np.concatenate([cos_hi[order], -sin_hi[order]]),
            np.concatenate([cos_lo[order], -sin_lo[order]]),
        ]
    )


def transform_call(own, pieces, first):
    vmem = pl.BlockSpec(memory_space=pltpu.VMEM)
    return pl.pallas_call(
        transform_kernel,
        out_shape=jax.ShapeDtypeStruct((4, 32, 8, G), jnp.float32),
        in_specs=[vmem] * 10,
        out_specs=pl.BlockSpec(memory_space=pl.ANY),
        scratch_shapes=[
            pltpu.VMEM((32 * 128, 128), jnp.float32),
            pltpu.VMEM((4, 4, 8, 8, G), jnp.float32),
            pltpu.SemaphoreType.DMA((4,)),
        ],
        compiler_params=pltpu.CompilerParams(vmem_limit_bytes=8 << 20),
        name="transform",
    )(own, *pieces, first)


def swap(x, axis, mask):
    count = lax.axis_size(axis)
    return lax.ppermute(x, axis, [(i, i ^ mask) for i in range(count)])


def flat(y, z, core, x):
    return ((y * 4 + z % 4) * 2 + core) * 8 + z // 4 * 4 + x


def plane_groups():
    return [
        [flat(y, z, core, x) for x in range(4) for z in range(8)] for y in range(4) for core in range(2)
    ]


def join_kernel(a_ref, b_ref, out_ref):
    size = a_ref.shape[1]
    out_ref[:, :size] = a_ref[...]
    out_ref[:, size:] = b_ref[...]


def join(a, b):
    vmem = pl.BlockSpec(memory_space=pltpu.VMEM)
    return pl.pallas_call(
        join_kernel,
        out_shape=jax.ShapeDtypeStruct((a.shape[0], 2 * a.shape[1]), jnp.float32),
        in_specs=[vmem, vmem],
        out_specs=vmem,
        compiler_params=pltpu.CompilerParams(vmem_limit_bytes=4 << 20),
        name="join",
    )(a, b)


def shards(coords, weights, thermal, angles, miller, observed):
    atom_count = lax.axis_size("atom")
    refl_count = lax.axis_size("refl")
    g = lax.axis_index("refl")
    j = lax.axis_index("atom")
    own_count = observed.shape[2]
    scales = (
        1.0 / math.sqrt(coords.shape[1] * atom_count),
        1.0 / math.sqrt(own_count * atom_count * refl_count),
    )
    atoms = jnp.concatenate([coords, weights[None], thermal[None], jnp.zeros_like(coords)], axis=0)
    atoms = join(atoms, swap(atoms, "atom", 1))

    sets = [
        lax.dynamic_slice_in_dim(miller[:, 0, :], (j ^ mask) * own_count, own_count, 1).astype(jnp.float32)
        for mask in (16, 20, 4, 0)
    ]
    indices = sets[3]
    sets = jnp.stack(sets)
    resolution = jnp.sum(sets * sets, axis=1) * (-LOG2E / (G * G))
    s2 = jnp.broadcast_to(resolution[:, :, None], (4, own_count, 128))
    lhs = jnp.transpose(sets, (0, 2, 1))[:, None, :, :, None] * jnp.eye(4, dtype=jnp.float32)[:, None, None, :]
    lhs = jnp.pad(lhs.reshape(4, 4 * own_count, 12), ((0, 0), (0, 0), (0, 4)))
    lhs = jnp.concatenate([lhs, lhs, lhs], axis=2).astype(jnp.bfloat16)
    rc = jnp.pad(jnp.tile(angles.T, (3, 1)), ((0, 4), (0, 0)))
    y, core = j // 8, j % 2
    own = jnp.stack([core, g, j, y]).astype(jnp.int32)
    own = jnp.broadcast_to(own[:, None], (4, 128))
    indices, observed, own, rc, atoms = lax.optimization_barrier(
        (indices, observed[:, 0, :], own, rc, atoms)
    )

    more = swap(atoms, "atom", 2)
    acc, rc = phase_call(lhs[:2], s2[:2], rc, atoms, 0, None, False)
    more, acc = lax.optimization_barrier((more, acc))
    atoms = join(atoms, more)
    more = swap(atoms, "atom", 8)
    (acc,) = phase_call(lhs[:2], s2[:2], rc, atoms, atoms.shape[1] // 2, acc, False)
    more, acc = lax.optimization_barrier((more, acc))
    atoms = join(atoms, more)
    (away,) = phase_call(lhs[:2], s2[:2], rc, atoms, atoms.shape[1] // 2, acc, True)
    near = swap(away, "atom", 16)
    (side,) = phase_call(lhs[2:3], s2[2:3], rc, atoms, 0, None, True)
    near, side = lax.optimization_barrier((near, side))
    across = swap(side + near[1:], "atom", 4)
    (here,) = phase_call(lhs[3:], s2[3:], rc, atoms, 0, None, True)
    across, here = lax.optimization_barrier((across, here))
    payload = coefficient_call(here, near, across, observed, indices, scales)

    plane = lax.all_to_all(
        payload, ("atom", "refl"), 0, 0, tiled=True, axis_index_groups=plane_groups()
    )
    planes = [plane] + [swap(plane, "atom", 8 * step) for step in range(1, 4)]
    planes += [swap(plane, "atom", 1) for plane in planes]
    lines = [scatter_call(q // 4, q % 4, own, plane) for q, plane in enumerate(planes)]
    return transform_call(own, lines, first_table())


def solution(mesh):
    placed = (
        P(None, "atom"),
        P("atom"),
        P("atom"),
        P(),
        P(None, "refl", None),
        P(None, "refl", "atom"),
    )
    return jax.shard_map(
        shards, mesh=mesh, in_specs=placed, out_specs=P(None, "refl", "atom", None), check_vma=False
    )
```
